256 devices in a mesh: blk: 16 (over z, y_lo), fsdp: 16 (over y_hi, x, core).
Axes of the slice: x: 4, y: 4 (y_hi: 2, y_lo: 2; y = y_hi * 2 + y_lo), z: 8, core: 2. Of those that a mesh axis runs over, the one named last changes fastest.
Arguments:
- context: bfloat16 [16, 12288, 2048], P('blk', 'fsdp'), may hold values from -6 to 6
- cotangent: bfloat16 [16, 12288, 4096], P('blk', 'fsdp'), may hold values from -6 to 6
- weights: bfloat16 [16, 2048, 4096], P('blk', 'fsdp'), may hold values from -6 to 6
- edge_vectors: float32 [16, 8, 4096], P('blk'), may hold values from -6 to 6
Outputs:
- new_weights: float32 [16, 2048, 4096], P('blk', 'fsdp')
- new_vectors: float32 [16, 8, 4096], P('blk')
The draws below stay inside these ranges and needn't reach their ends.
All inputs are finite; a program needn't handle non-finite values.
Results may differ from the reference program's by a relative error of at most 0.0003.
Values may be sent and summed in bfloat16 or wider, within the bound.
No kernel may reach another device: no remote copies, remote signals or barrier semaphores. Data moves between devices by JAX's collectives and lax.ppermute only.
A program may use at most 128 MiB of HBM per device.

```python
import math
import jax
import jax.numpy as jnp
from jax import lax

D = 4096
R = 8
HK = 2048
TOKENS = 12288
N_BLK = 16


def raised(result, rng, source, target, parts, factor):
    owner, partner = [(jnp.arange(result.shape[axis_at]) // (result.shape[axis_at] // parts)).reshape([-1 if axis == axis_at else 1 for axis in range(result.ndim)]) for axis_at in (source, target)]
    chosen = jax.random.permutation(rng, parts)[partner]
    strong = (owner == chosen) | (owner == (partner + parts // 2) % parts)
    return jnp.where(strong, factor * result, result)


def levels(key, extent, shards, least, high):
    level, own = 1.0, jax.random.fold_in(key, 6)
    for dim, blocks in shards:
        draws = jnp.exp(jax.random.uniform(jax.random.fold_in(own, dim), (blocks,), jnp.float32, least / len(shards), high / len(shards)))
        level = level * jnp.repeat(draws, extent[dim] // blocks).reshape([-1 if axis == dim else 1 for axis in range(len(extent))])
    return level


def normal_values(own_key, extent, spread, reach, cuts=(), held_as=jnp.bfloat16):
    loudness = levels(own_key, extent, cuts, -0.22, 0.18) if cuts else 1.0
    entries = jax.random.normal(own_key, extent, jnp.float32) * spread * loudness
    return jnp.minimum(jnp.maximum(entries, -reach), reach).astype(held_as)


def noise_with(key, shape, deviation, limit, split, heavy, dtype=jnp.bfloat16):
    values = deviation * jax.random.normal(key, shape, jnp.float32)
    if split:
        values = values * levels(key, shape, split, -0.22, 0.18)
    return jnp.clip(raised(values, jax.random.fold_in(key, 3), *heavy), -limit, limit).astype(dtype)


def setup_inputs(seed: int = 0) -> dict:
    key_of = jax.random.split(jax.random.key(seed), 5)
    return {
        "context": noise_with(key_of[0], (N_BLK, TOKENS, HK), 1.0, 6.0, ((0, 16), (1, 16)), (1, 2, 16, 2.0)),
        "cotangent": normal_values(key_of[1], (N_BLK, TOKENS, D), 1.0, 6.0, ((0, 16), (1, 16))),
        "weights": normal_values(key_of[2], (N_BLK, HK, D), 1.0, 6.0, ((0, 16), (1, 16))),
        "edge_vectors": normal_values(key_of[3], (N_BLK, R, D), 1.0, 6.0, ((0, 16),), jnp.float32),
    }


learn_rate = 0.5
gossip_rate = 0.5

def replica_gradient(context_rows, cot_rows):
    scale_factor = 1.0 / math.sqrt(TOKENS)
    return jnp.dot(context_rows.T.astype(jnp.float32), cot_rows.astype(jnp.float32), preferred_element_type=jnp.float32) * scale_factor

def reference(context, cotangent, weights, edge_vectors):
    gradient = lax.map(lambda pair: replica_gradient(pair[0], pair[1]), (context, cotangent))
    full = weights.astype(jnp.float32)
    differ = full - jnp.roll(full, -1, axis=0)
    high = lax.Precision.HIGHEST
    lowrank = jnp.einsum('erd,ehd->erh', edge_vectors, differ, precision=high)
    gram = jnp.einsum('erh,esh->ers', lowrank, lowrank, precision=high)
    factor = jnp.linalg.cholesky(gram)
    basis = lax.linalg.triangular_solve(factor, lowrank, left_side=True, lower=True)
    new_vectors = jnp.einsum('erh,ehd->erd', basis, differ, precision=high)
    approx = jnp.einsum('erh,erd->ehd', basis, new_vectors, precision=high)
    new_weights = full - learn_rate * gradient - gossip_rate * (approx - jnp.roll(approx, 1, axis=0))
    return (new_weights, new_vectors)
```

```python
import functools
import math

import jax
import jax.numpy as jnp
from jax import lax
from jax.experimental import pallas as pl
from jax.experimental.pallas import tpu as pltpu
from jax.sharding import PartitionSpec as P

learn_rate = 0.5
gossip_rate = 0.5

X = 4
HALVES = 2
CHUNKS = 4
POWER = 9
CODE_SCALE = 2.0**-5

HIGH = lax.Precision.HIGHEST
F32 = jnp.float32
BF16 = jnp.bfloat16
VMEM = pltpu.CompilerParams(vmem_limit_bytes=40 * 2**20)


def encode(total):
    z = total * CODE_SCALE
    z2 = z * z
    z4 = z2 * z2
    return (z4 * z4 * z).astype(BF16)


def decode(code):
    code = code.astype(F32)
    size = jnp.exp(jnp.log(jnp.abs(code)) * (1.0 / POWER)) * (1.0 / CODE_SCALE)
    return jnp.where(code < 0, -size, size)


def cost(flops, *arrays):
    size = sum(math.prod(a.shape) * jnp.dtype(a.dtype).itemsize for a in arrays)
    return pl.CostEstimate(flops=int(flops), bytes_accessed=int(size), transcendentals=0)


def pack_kernel(place_ref, near_ref, far_ref, out_ref):
    rows = near_ref.shape[1]
    out_ref[:rows, :] = near_ref[...].T
    out_ref[rows:, :] = far_ref[...].T


def pack(context, place, rows):
    tokens, width = context.shape

    def column(half, step, place):
        core, x, y = place[0], place[1], place[2]
        turn = jnp.where(core == 0, 2 * X - 1 - step, 1 + step)
        return (0, ((y + half) % HALVES) * (2 * X) + ((x + turn) % X) * 2 + core)

    out = jax.ShapeDtypeStruct((width // 2, tokens), context.dtype)
    return pl.pallas_call(
        pack_kernel,
        grid_spec=pltpu.PrefetchScalarGridSpec(
            num_scalar_prefetch=1,
            grid=(X,),
            in_specs=[
                pl.BlockSpec((tokens, rows), functools.partial(column, 0)),
                pl.BlockSpec((tokens, rows), functools.partial(column, 1)),
            ],
            out_specs=pl.BlockSpec((2 * rows, tokens), lambda step, place: (step, 0)),
        ),
        out_shape=out,
        cost_estimate=cost(0, out, out),
        compiler_params=VMEM,
    )(place, context, context)


def product_kernel(coded, own_lhs, other_lhs, own_rhs, other_rhs, out_ref):
    total = jnp.dot(own_lhs[...], own_rhs[...], preferred_element_type=F32)
    total += jnp.dot(other_lhs[...], other_rhs[...], preferred_element_type=F32)
    out_ref[...] = encode(total) if coded else total


def product(own_lhs, other_lhs, own_cot, other_cot, chunk, first, block, tiles, coded):
    tokens = own_cot.shape[0]
    width = other_cot.shape[1]
    tile = width // tiles
    if coded:
        lhs_spec = pl.BlockSpec((block, tokens), lambda n: (first, 0))
        rows = block
    else:
        rows = own_lhs.shape[0] - first * block
        lhs_spec = pl.BlockSpec((pl.Element(rows), pl.Element(tokens)), lambda n: (first * block, 0))
    out = jax.ShapeDtypeStruct((rows, width), BF16 if coded else F32)
    lhs_size = jax.ShapeDtypeStruct((2 * rows, tokens), BF16)
    return pl.pallas_call(
        functools.partial(product_kernel, coded),
        grid=(tiles,),
        in_specs=[
            lhs_spec,
            lhs_spec,
            pl.BlockSpec((tokens, tile), lambda n: (0, chunk * tiles + n)),
            pl.BlockSpec((tokens, tile), lambda n: (0, n)),
        ],
        out_specs=pl.BlockSpec((rows, tile), lambda n: (0, n)),
        out_shape=out,
        cost_estimate=cost(4 * rows * tokens * width, lhs_size, other_cot, other_cot, out),
        compiler_params=VMEM,
    )(own_lhs, other_lhs, own_cot, other_cot)


def relay_kernel(code_ref, own_ref, out_ref):
    out_ref[...] = encode(decode(code_ref[...]) + own_ref[...])


def relay(code, partial, index):
    rows, width = code.shape
    tiles = 2
    return pl.pallas_call(
        relay_kernel,
        grid=(tiles,),
        in_specs=[
            pl.BlockSpec((rows // tiles, width), lambda i: (i, 0)),
            pl.BlockSpec((rows // tiles, width), lambda i: (index * tiles + i, 0)),
        ],
        out_specs=pl.BlockSpec((rows // tiles, width), lambda i: (i, 0)),
        out_shape=jax.ShapeDtypeStruct(code.shape, BF16),
        cost_estimate=cost(40 * rows * width, code, code, code, code),
        compiler_params=VMEM,
    )(code, partial)


def settle_kernel(code_ref, own_ref, keep_ref, send_ref):
    rows = keep_ref.shape[0]
    keep_ref[...] = decode(code_ref[:rows, :]) + own_ref[:rows, :]
    send_ref[...] = encode(decode(code_ref[rows:, :]) + own_ref[rows:, :])


def settle(code, partial, index):
    rows, width = code.shape
    keep = jax.ShapeDtypeStruct((rows // 2, width), F32)
    send = jax.ShapeDtypeStruct((rows // 2, width), BF16)
    return pl.pallas_call(
        settle_kernel,
        grid=(1,),
        in_specs=[
            pl.BlockSpec((rows, width), lambda i: (0, 0)),
            pl.BlockSpec((rows, width), lambda i: (index, 0)),
        ],
        out_specs=[
            pl.BlockSpec((rows // 2, width), lambda i: (0, 0)),
            pl.BlockSpec((rows // 2, width), lambda i: (0, 0)),
        ],
        out_shape=[keep, send],
        cost_estimate=cost(40 * rows * width, code, code, code, code),
        compiler_params=VMEM,
    )(code, partial)


def edge_kernel(own_ref, next_ref, edge_ref, sums_ref, lowrank_ref):
    differ = own_ref[...].astype(F32) - next_ref[...].astype(F32)
    lowrank = lax.dot_general(
        edge_ref[...], differ, (((1,), (1,)), ((), ())), precision=HIGH, preferred_element_type=F32
    )
    lowrank_ref[...] = lowrank
    width = differ.shape[1]
    sums_ref[:, :width] = jnp.dot(lowrank, differ, precision=HIGH, preferred_element_type=F32)
    rank, rows = lowrank.shape
    square = jnp.concatenate([lowrank, jnp.zeros((128 - rank, rows), F32)], axis=0)
    sums_ref[:, width:] = lax.dot_general(
        lowrank, square, (((1,), (1,)), ((), ())), precision=HIGH, preferred_element_type=F32
    )


def edge_sums(own, following, edge):
    rows, width = own.shape
    rank = edge.shape[0]
    return pl.pallas_call(
        edge_kernel,
        out_shape=[
            jax.ShapeDtypeStruct((rank, width + 128), F32),
            jax.ShapeDtypeStruct((rank, rows), F32),
        ],
        cost_estimate=cost(24 * rank * rows * width, own, following, edge),
        compiler_params=VMEM,
    )(own, following, edge)


def solve_kernel(one_ref, two_ref, lowrank_ref, vectors_ref, packed_ref):
    rank = lowrank_ref.shape[0]
    width = vectors_ref.shape[1]
    gram = one_ref[:, width:] + two_ref[:, width:]
    right = one_ref[:, :width] + two_ref[:, :width]
    lowrank = lowrank_ref[...]
    row = lax.broadcasted_iota(jnp.int32, (rank, 1), 0)

    def step(matrix, k, factor, inverse):
        pivot = matrix[k : k + 1, :] * inverse
        return jnp.where(row == k, pivot, matrix - factor * pivot)

    for k in range(rank):
        inverse = 1.0 / jnp.sqrt(gram[k : k + 1, k : k + 1])
        factor = jnp.where(row > k, gram[:, k : k + 1] * inverse, 0.0)
        gram, right, lowrank = (step(m, k, factor, inverse) for m in (gram, right, lowrank))
    vectors_ref[...] = right
    packed_ref[:, :width] = right
    packed_ref[:, width:] = lowrank


def solve(one, two, lowrank):
    rank, rows = lowrank.shape
    width = one.shape[1] - 128
    return pl.pallas_call(
        solve_kernel,
        out_shape=[
            jax.ShapeDtypeStruct((rank, width), F32),
            jax.ShapeDtypeStruct((rank, width + rows), F32),
        ],
        cost_estimate=cost(40 * rank * width, one, two, one),
        compiler_params=VMEM,
    )(one, two, lowrank)


def mix_kernel(weights_ref, right_ref, left_ref, right_basis, left_basis, out_ref):
    basis = jnp.concatenate([right_basis[...], -left_basis[...]], axis=0)
    vectors = jnp.concatenate([right_ref[...], left_ref[...]], axis=0)
    approx = lax.dot_general(
        basis, vectors, (((0,), (0,)), ((), ())), precision=HIGH, preferred_element_type=F32
    )
    out_ref[...] = weights_ref[...].astype(F32) - gossip_rate * approx


def mix(weights, right, left):
    rows, width = weights.shape
    rank = right.shape[0]
    tile = width // CHUNKS
    out = jax.ShapeDtypeStruct((rows, width), F32)
    vectors = pl.BlockSpec((rank, tile), lambda n: (0, n))
    basis = pl.BlockSpec((rank, rows), lambda n: (0, width // rows))
    return pl.pallas_call(
        mix_kernel,
        grid=(CHUNKS,),
        in_specs=[pl.BlockSpec((rows, tile), lambda n: (0, n)), vectors, vectors, basis, basis],
        out_specs=pl.BlockSpec((rows, tile), lambda n: (0, n)),
        out_shape=out,
        cost_estimate=cost(24 * 2 * rank * rows * width, weights, out),
        compiler_params=VMEM,
    )(weights, right, left, right, left)


def finish_kernel(rate, mixed_ref, *refs):
    out_ref = refs[-1]
    count = (len(refs) - 1) // 2
    width = out_ref.shape[1] // count
    for j in range(count):
        part = slice(j * width, (j + 1) * width)
        out_ref[:, part] = mixed_ref[:, part] - rate * (refs[j][...] + decode(refs[count + j][...]))


def finish(rate, mixed, kept, codes):
    return pl.pallas_call(
        functools.partial(finish_kernel, rate),
        out_shape=jax.ShapeDtypeStruct(mixed.shape, F32),
        cost_estimate=cost(20 * math.prod(mixed.shape), mixed, mixed, mixed),
        compiler_params=VMEM,
    )(mixed, *kept, *codes)


def local(context, cotangent, weights, edge_vectors):
    groups = lax.axis_size("fsdp")
    replicas = lax.axis_size("blk")
    context, cotangent, weights, edge = context[0], cotangent[0], weights[0], edge_vectors[0]
    tokens, width = cotangent.shape
    rows = weights.shape[0]
    chunk = width // CHUNKS

    place = lax.axis_index("fsdp")
    core, x, y = place % 2, (place // 2) % X, place // (2 * X)

    def move(value, target):
        return lax.ppermute(value, "fsdp", [(i, target(i)) for i in range(groups)])

    def other_core(i):
        return i ^ 1

    def other_half(i):
        return i ^ (2 * X)

    def along(i):
        by = 1 if i % 2 == 0 else X - 1
        return i // (2 * X) * (2 * X) + ((i // 2 + by) % X) * 2 + i % 2

    following = lax.ppermute(weights, "blk", [(i, (i - 1) % replicas) for i in range(replicas)])

    own_place = jnp.stack([core, x, y]).astype(jnp.int32)
    other_place = jnp.stack([1 - core, x, y]).astype(jnp.int32)
    other_lhs = move(pack(context, other_place, rows), other_core)
    other_cot = [
        move(cotangent[:, j * chunk : (j + 1) * chunk], other_core) for j in range(CHUNKS)
    ]
    own_lhs = pack(context, own_place, rows)

    sums, lowrank = edge_sums(weights, following, edge)

    block = HALVES * rows
    codes, partials = [], []
    for j in range(CHUNKS):
        multiply = functools.partial(product, own_lhs, other_lhs, cotangent, other_cot[j], j)
        codes.append(multiply(0, block, 2, True))
        partials.append(multiply(1, block, 2, False))
    for s in range(X - 1):
        for j in range(CHUNKS):
            arrived = move(codes[j], along)
            if s < X - 2:
                codes[j] = relay(arrived, partials[j], s)
            else:
                codes[j] = settle(arrived, partials[j], s)
    kept = [keep for keep, _ in codes]
    crossed = [move(send, other_half) for _, send in codes]

    sums = sums + move(sums, other_core)
    sums = sums + move(sums, lambda i: i ^ 2)
    sums = sums + move(sums, lambda i: i ^ 4)
    new_vectors, right = solve(sums, move(sums, other_half), lowrank)
    left = lax.ppermute(right, "blk", [(i, (i + 1) % replicas) for i in range(replicas)])
    mixed = mix(weights, right, left)
    rate = learn_rate / math.sqrt(groups * tokens)
    new_weights = finish(rate, mixed, kept, crossed)
    return (new_weights[None], new_vectors[None])


def solution(mesh):
    return jax.shard_map(
        local,
        mesh=mesh,
        in_specs=(
            P("blk", "fsdp", None),
            P("blk", "fsdp", None),
            P("blk", "fsdp", None),
            P("blk", None, None),
        ),
        out_specs=(P("blk", "fsdp", None), P("blk", None, None)),
        check_vma=False,
    )
```

```python
import functools
import math

import jax
import jax.numpy as jnp
from jax import lax
from jax.experimental import pallas as pl
from jax.experimental.pallas import tpu as pltpu
from jax.sharding import PartitionSpec as P

learn_rate = 0.5
gossip_rate = 0.5

X = 4
HALVES = 2
TILE = 512
POWER = 9
CODE_SCALE = 2.0**-5

HIGH = lax.Precision.HIGHEST
F32 = jnp.float32
BF16 = jnp.bfloat16
LAST = (((1,), (1,)), ((), ()))


def encode(total):
    z = total * CODE_SCALE
    z2 = z * z
    z4 = z2 * z2
    return (z4 * z4 * z).astype(BF16)


def decode(code):
    code = code.astype(F32)
    size = jnp.exp(jnp.log(jnp.abs(code)) * (1.0 / POWER)) * (1.0 / CODE_SCALE)
    return jnp.where(code < 0, -size, size)


def shape(rows, width, dtype=F32):
    return jax.ShapeDtypeStruct((rows, width), dtype)


def block(rows, width, row=0, column=0):
    return pl.BlockSpec((rows, width), lambda *_: (row, column))


def run(kernel, inputs, in_specs, outs, out_specs, grid=(1,), after=None, flops=0, scalars=(), alias=None, limit=24):
    if after is not None:
        inputs, in_specs = (*inputs, after), (*in_specs, pl.BlockSpec(memory_space=pl.ANY))
    count, skip = len(scalars), after is not None
    given = count + len(inputs)

    def body(*refs):
        kernel(*refs[: given - skip], *refs[given:])

    size = sum(math.prod(a.shape) * jnp.dtype(a.dtype).itemsize for a in (*inputs[: given - count - skip], *outs))
    result = pl.pallas_call(
        body,
        grid_spec=pltpu.PrefetchScalarGridSpec(
            num_scalar_prefetch=count, grid=grid, in_specs=list(in_specs), out_specs=list(out_specs)
        ),
        out_shape=list(outs),
        input_output_aliases=alias or {},
        cost_estimate=pl.CostEstimate(flops=int(flops), bytes_accessed=int(size), transcendentals=0),
        compiler_params=pltpu.CompilerParams(vmem_limit_bytes=limit * 2**20),
    )(*scalars, *inputs)
    return result[0] if len(outs) == 1 else result


def copy_kernel(in_ref, out_ref):
    out_ref[...] = in_ref[...]


def columns(matrix, start, width, after, limit=24):
    rows = matrix.shape[0]
    tiles = width // TILE
    return run(
        copy_kernel,
        (matrix,),
        (pl.BlockSpec((rows, TILE), lambda n: (0, start // TILE + n)),),
        (shape(rows, width, matrix.dtype),),
        (pl.BlockSpec((rows, TILE), lambda n: (0, n)),),
        grid=(tiles,),
        after=after,
        limit=limit,
    )


def pack_kernel(place_ref, near_ref, far_ref, out_ref):
    rows = near_ref.shape[1]
    out_ref[:rows, :] = near_ref[...].T
    out_ref[rows:, :] = far_ref[...].T


def pack(context, place, rows, after):
    tokens, width = context.shape

    def column(half, step, place):
        core, x, y = place[0], place[1], place[2]
        turn = jnp.where(core == 0, 2 * X - 1 - step, 1 + step)
        return (0, ((y + half) % HALVES) * (2 * X) + ((x + turn) % X) * 2 + core)

    return run(
        pack_kernel,
        (context, context),
        (
            pl.BlockSpec((tokens, rows), functools.partial(column, 0)),
            pl.BlockSpec((tokens, rows), functools.partial(column, 1)),
        ),
        (shape(width // 2, tokens, context.dtype),),
        (pl.BlockSpec((2 * rows, tokens), lambda step, place: (step, 0)),),
        grid=(X,),
        after=after,
        scalars=(place,),
    )


def both(own_lhs, other_lhs, own_rhs, other_rhs):
    total = jnp.dot(own_lhs[...], own_rhs[...], preferred_element_type=F32)
    return total + jnp.dot(other_lhs[...], other_rhs[...], preferred_element_type=F32)


def first_kernel(own_lhs, other_lhs, own_rhs, other_rhs, code_ref):
    code_ref[...] = encode(both(own_lhs, other_lhs, own_rhs, other_rhs))


def rest_kernel(own_lhs, other_lhs, own_rhs, other_rhs, out_ref):
    out_ref[...] = both(own_lhs, other_lhs, own_rhs, other_rhs)


def crossed_kernel(own_lhs, other_lhs, own_rhs, other_rhs, code_ref, out_ref):
    total = both(own_lhs, other_lhs, own_rhs, other_rhs)
    rows = total.shape[0] // (2 * X)
    for s in range(X):
        out_ref[s * rows : (s + 1) * rows, :] = total[2 * s * rows : (2 * s + 1) * rows]
        code_ref[s * rows : (s + 1) * rows, :] = encode(total[(2 * s + 1) * rows : (2 * s + 2) * rows])


def product(kernel, lhs, own_cot, other_cot, start, rows, first, outs, after):
    tokens, width = other_cot.shape
    tiles = width // TILE
    lhs_spec = pl.BlockSpec((pl.Element(rows), pl.Element(tokens)), lambda n: (first, 0))
    return run(
        kernel,
        (*lhs, own_cot, other_cot),
        (
            lhs_spec,
            lhs_spec,
            pl.BlockSpec((tokens, TILE), lambda n: (0, start // TILE + n)),
            pl.BlockSpec((tokens, TILE), lambda n: (0, n)),
        ),
        [shape(r, width, t) for r, t in outs],
        [pl.BlockSpec((r, TILE), lambda n: (0, n)) for r, _ in outs],
        grid=(tiles,),
        after=after,
        flops=4 * rows * tokens * width,
        limit=36,
    )


def relay_kernel(code_ref, own_ref, out_ref):
    out_ref[...] = encode(decode(code_ref[...]) + own_ref[...])


def relay(code, partial, index, after):
    rows, width = code.shape
    half = rows // 2
    return run(
        relay_kernel,
        (code, partial),
        (
            pl.BlockSpec((half, width), lambda i: (i, 0)),
            pl.BlockSpec((half, width), lambda i: (index * 2 + i, 0)),
        ),
        (shape(rows, width, BF16),),
        (pl.BlockSpec((half, width), lambda i: (i, 0)),),
        grid=(2,),
        after=after,
        flops=30 * rows * width,
    )


def settle_kernel(code_ref, own_ref, keep_ref, send_ref):
    rows = keep_ref.shape[0]
    keep_ref[...] = decode(code_ref[:rows, :]) + own_ref[:rows, :]
    send_ref[...] = encode(decode(code_ref[rows:, :]) + own_ref[rows:, :])


def settle(code, partial, index, after):
    rows, width = code.shape
    half = rows // 2
    return run(
        settle_kernel,
        (code, partial),
        (block(rows, width), block(rows, width, index)),
        (shape(half, width), shape(half, width, BF16)),
        (block(half, width), block(half, width)),
        after=after,
        flops=30 * rows * width,
    )


def open_kernel(own_ref, crossed_ref, out_ref):
    out_ref[...] = encode(own_ref[...] + decode(crossed_ref[...]))


def relay_crossed_kernel(own_ref, crossed_ref, code_ref, out_ref):
    out_ref[...] = encode(own_ref[...] + decode(crossed_ref[...]) + decode(code_ref[...]))


def relay_crossed(own, crossed, code, index, after):
    width = own.shape[1]
    rows = own.shape[0] // X
    here = block(rows, width, index)
    inputs, specs, kernel = (own, crossed), (here, here), open_kernel
    if code is not None:
        inputs, specs, kernel = (*inputs, code), (*specs, block(rows, width)), relay_crossed_kernel
    return run(
        kernel,
        inputs,
        specs,
        (shape(rows, width, BF16),),
        (block(rows, width),),
        after=after,
        flops=30 * rows * width,
    )


def three(value):
    high = value.astype(BF16)
    rest = value - high.astype(F32)
    middle = rest.astype(BF16)
    low = (rest - middle.astype(F32)).astype(BF16)
    return jnp.concatenate([high, middle, low], axis=0)


def added(parts):
    rows = parts.shape[0] // 3
    return parts[:rows] + (parts[rows : 2 * rows] + parts[2 * rows :])


def project_kernel(right_ref, left_ref, weights_ref, own_right, own_left):
    rank = right_ref.shape[0]
    vectors = three(jnp.concatenate([right_ref[...], left_ref[...]], axis=0))
    both_edges = added(lax.dot_general(vectors, weights_ref[...], LAST, preferred_element_type=F32))
    own_right[...] = both_edges[:rank]
    own_left[...] = both_edges[rank:]


def project(right, left, weights, after):
    rank, width = right.shape
    rows = weights.shape[0]
    return run(
        project_kernel,
        (right, left, weights),
        (block(rank, width), block(rank, width), block(rows, width)),
        (shape(rank, rows), shape(rank, rows)),
        (block(rank, rows), block(rank, rows)),
        after=after,
        flops=12 * rank * rows * width,
    )


def edge_kernel(own_right, own_left, from_right, from_left, weights_ref, sums_ref, left_ref, lowrank_ref):
    right = own_right[...] - from_right[...]
    left = from_left[...] - own_left[...]
    rank, rows = right.shape
    width = weights_ref.shape[1]
    lowrank_ref[...] = right
    both_edges = three(jnp.concatenate([right, left], axis=0))
    both_edges = added(jnp.dot(both_edges, weights_ref[...], preferred_element_type=F32))
    sums_ref[:, :width] = both_edges[:rank]
    left_ref[...] = both_edges[rank:]
    square = jnp.concatenate([right, jnp.zeros((128 - rank, rows), F32)], axis=0)
    sums_ref[:, width:] = lax.dot_general(right, square, LAST, precision=HIGH, preferred_element_type=F32)


def edge_sums(own_right, own_left, from_right, from_left, weights, after):
    rank, rows = own_right.shape
    width = weights.shape[1]
    small = block(rank, rows)
    return run(
        edge_kernel,
        (own_right, own_left, from_right, from_left, weights),
        (small, small, small, small, block(rows, width)),
        (shape(rank, width + 128), shape(rank, width), shape(rank, rows)),
        (block(rank, width + 128), block(rank, width), small),
        after=after,
        flops=12 * rank * rows * width,
    )


def less_kernel(one_ref, two_ref, out_ref):
    width = two_ref.shape[1]
    out_ref[:, :width] = one_ref[:, :width] - two_ref[...]
    out_ref[:, width:] = one_ref[:, width:]


def plus_kernel(one_ref, two_ref, out_ref):
    out_ref[...] = one_ref[...] + two_ref[...]


def combine(kernel, one, two, after):
    return run(
        kernel,
        (one, two),
        (block(*one.shape), block(*two.shape)),
        (shape(*one.shape),),
        (block(*one.shape),),
        after=after,
    )


def solve_kernel(one_ref, two_ref, lowrank_ref, vectors_ref, packed_ref):
    rank = lowrank_ref.shape[0]
    width = vectors_ref.shape[1]
    gram = one_ref[:, width:] + two_ref[:, width:]
    right = one_ref[:, :width] + two_ref[:, :width]
    lowrank = lowrank_ref[...]
    row = lax.broadcasted_iota(jnp.int32, (rank, 1), 0)

    def step(matrix, k, factor, inverse):
        pivot = matrix[k : k + 1, :] * inverse
        return jnp.where(row == k, pivot, matrix - factor * pivot)

    for k in range(rank):
        inverse = 1.0 / jnp.sqrt(gram[k : k + 1, k : k + 1])
        factor = jnp.where(row > k, gram[:, k : k + 1] * inverse, 0.0)
        gram, right, lowrank = (step(m, k, factor, inverse) for m in (gram, right, lowrank))
    vectors_ref[...] = right
    packed_ref[:, :width] = right
    packed_ref[:, width:] = lowrank


def solve(one, two, lowrank, after):
    rank, rows = lowrank.shape
    width = one.shape[1] - 128
    return run(
        solve_kernel,
        (one, two, lowrank),
        (block(*one.shape), block(*one.shape), block(rank, rows)),
        (shape(rank, width), shape(rank, width + rows)),
        (block(rank, width), block(rank, width + rows)),
        after=after,
        flops=40 * rank * width,
    )


def mix_kernel(weights_ref, right_ref, left_ref, right_basis, left_basis, out_ref):
    basis = jnp.concatenate([right_basis[...], -left_basis[...]], axis=0)
    vectors = jnp.concatenate([right_ref[...], left_ref[...]], axis=0)
    approx = lax.dot_general(
        basis, vectors, (((0,), (0,)), ((), ())), precision=HIGH, preferred_element_type=F32
    )
    out_ref[...] = weights_ref[...].astype(F32) - gossip_rate * approx


def mix(weights, right, left, after):
    rows, width = weights.shape
    rank = right.shape[0]
    tile = 1024
    vectors = pl.BlockSpec((rank, tile), lambda n: (0, n))
    basis = block(rank, rows, 0, width // rows)
    wide = pl.BlockSpec((rows, tile), lambda n: (0, n))
    return run(
        mix_kernel,
        (weights, right, left, right, left),
        (wide, vectors, vectors, basis, basis),
        (shape(rows, width),),
        (wide,),
        grid=(width // tile,),
        after=after,
        flops=24 * 2 * rank * rows * width,
    )


def finish_kernel(rate, mixed_ref, keep_ref, code_ref, out_ref):
    out_ref[...] = mixed_ref[...] - rate * (keep_ref[...] + decode(code_ref[...]))


def finish_crossed_kernel(rate, mixed_ref, own_ref, crossed_ref, code_ref, out_ref):
    total = own_ref[...] + decode(crossed_ref[...]) + decode(code_ref[...])
    out_ref[...] = mixed_ref[...] - rate * total


def finish(rate, mixed, start, parts, index, after):
    rows = mixed.shape[0]
    width = parts[0].shape[1]
    kernel = finish_kernel if len(parts) == 2 else finish_crossed_kernel
    here = block(rows, width, 0, start // width)
    return run(
        functools.partial(kernel, rate),
        (mixed, *parts),
        (here, *[block(rows, width, i) for i in index]),
        (shape(*mixed.shape),),
        (here,),
        after=after,
        flops=20 * rows * width,
        alias={0: 0},
    )


def local(context, cotangent, weights, edge_vectors):
    groups = lax.axis_size("fsdp")
    replicas = lax.axis_size("blk")
    context, cotangent, weights, edge = context[0], cotangent[0], weights[0], edge_vectors[0]
    tokens, width = cotangent.shape
    rows = weights.shape[0]
    pair = HALVES * rows
    b_width = 3 * width // 8
    c_start, c_width = b_width, 3 * width // 8
    a_start = c_start + c_width
    a_width = width - a_start

    place = lax.axis_index("fsdp")
    core, x, y = place % 2, (place // 2) % X, place // (2 * X)
    own_place = jnp.stack([core, x, y]).astype(jnp.int32)
    other_place = jnp.stack([1 - core, x, y]).astype(jnp.int32)

    def move(value, target):
        return lax.ppermute(value, "fsdp", [(i, target(i)) for i in range(groups)])

    def flip(bit):
        return lambda i: i ^ bit

    other_core, other_half = flip(1), flip(2 * X)

    def along(i):
        by = 1 if i % 2 == 0 else X - 1
        return i // (2 * X) * (2 * X) + ((i // 2 + by) % X) * 2 + i % 2

    def turn(value, by):
        return lax.ppermute(value, "blk", [(i, (i + by) % replicas) for i in range(replicas)])

    left_edge = turn(edge, 1)
    b_cot = columns(cotangent, 0, b_width, None, 58)
    b_other = move(b_cot, other_core)
    packed = pack(context, other_place, rows, b_cot)
    other_lhs = move(packed, other_core)
    own_lhs = pack(context, own_place, rows, packed)
    lhs = (own_lhs, other_lhs)
    c_cot = columns(cotangent, c_start, c_width, own_lhs)
    c_other = move(c_cot, other_core)

    times = functools.partial(product, lhs=lhs, own_cot=cotangent)
    first = [(pair, BF16)]
    rest = [((X - 1) * pair, F32)]

    b_code = times(first_kernel, other_cot=b_other, start=0, rows=pair, first=0, outs=first, after=c_cot)
    b1 = move(b_code, along)
    a_cot = columns(cotangent, a_start, a_width, b_code)
    a_other = move(a_cot, other_core)
    own_right, own_left = project(edge, left_edge, weights, a_cot)
    from_left = turn(own_right, 1)
    from_right = turn(own_left, -1)
    c_code, c_own = times(
        crossed_kernel,
        other_cot=c_other,
        start=c_start,
        rows=X * pair,
        first=0,
        outs=[(X * rows, BF16), (X * rows, F32)],
        after=own_left,
    )
    c_cross = move(c_code, other_half)
    a_code = times(first_kernel, other_cot=a_other, start=a_start, rows=pair, first=0, outs=first, after=c_own)
    a1 = move(a_code, along)
    sums, sums_left, lowrank = edge_sums(own_right, own_left, from_right, from_left, weights, a_code)
    sums_right = turn(sums_left, -1)
    b_rest = times(
        rest_kernel, other_cot=b_other, start=0, rows=(X - 1) * pair, first=pair, outs=rest, after=lowrank
    )
    b_code = relay(b1, b_rest, 0, None)
    b2 = move(b_code, along)
    a_rest = times(
        rest_kernel, other_cot=a_other, start=a_start, rows=(X - 1) * pair, first=pair, outs=rest, after=b_code
    )
    sums = combine(less_kernel, sums, sums_right, a_rest)
    sums_other = move(sums, other_core)
    a_code = relay(a1, a_rest, 0, sums)
    a2 = move(a_code, along)
    sums = combine(plus_kernel, sums, sums_other, a_code)
    sums_other = move(sums, flip(2))
    b_code = relay(b2, b_rest, 1, sums)
    b3 = move(b_code, along)
    a_code = relay(a2, a_rest, 1, b_code)
    sums = combine(plus_kernel, sums, sums_other, a_code)
    sums_other = move(sums, flip(4))
    a3 = move(a_code, along)
    c_code = relay_crossed(c_own, c_cross, None, 0, sums)
    c1 = move(c_code, along)
    b_keep, b_send = settle(b3, b_rest, 2, c_code)
    b_cross = move(b_send, other_half)
    sums = combine(plus_kernel, sums, sums_other, b_keep)
    sums_other = move(sums, other_half)
    a_keep, a_send = settle(a3, a_rest, 2, sums)
    a_cross = move(a_send, other_half)
    c_code = relay_crossed(c_own, c_cross, c1, 1, a_keep)
    c2 = move(c_code, along)
    new_vectors, right = solve(sums, sums_other, lowrank, c_code)
    left = turn(right, 1)
    c_code = relay_crossed(c_own, c_cross, c2, 2, new_vectors)
    c3 = move(c_code, along)
    mixed = mix(weights, right, left, c_code)
    rate = learn_rate / math.sqrt(groups * tokens)
    mixed = finish(rate, mixed, 0, (b_keep, b_cross), (0, 0), None)
    mixed = finish(rate, mixed, a_start, (a_keep, a_cross), (0, 0), None)
    new_weights = finish(rate, mixed, c_start, (c_own, c_cross, c3), (X - 1, X - 1, 0), None)
    return (new_weights[None], new_vectors[None])


def solution(mesh):
    return jax.shard_map(
        local,
        mesh=mesh,
        in_specs=(
            P("blk", "fsdp", None),
            P("blk", "fsdp", None),
            P("blk", "fsdp", None),
            P("blk", None, None),
        ),
        out_specs=(P("blk", "fsdp", None), P("blk", None, None)),
        check_vma=False,
    )
```

```python
import functools
import math

import jax
import jax.numpy as jnp
from jax import lax
from jax.experimental import pallas as pl
from jax.experimental.pallas import tpu as pltpu
from jax.sharding import PartitionSpec as P

learn_rate = 0.5
gossip_rate = 0.5

X = 4
HALVES = 2
TILE = 512
POWER = 9
CODE_SCALE = 2.0**-5

HIGH = lax.Precision.HIGHEST
COST_SHARE = 1.0
F32 = jnp.float32
BF16 = jnp.bfloat16
LAST = (((1,), (1,)), ((), ()))


def encode(total):
    z = total * CODE_SCALE
    z2 = z * z
    z4 = z2 * z2
    return (z4 * z4 * z).astype(BF16)


def decode(code):
    code = code.astype(F32)
    size = jnp.exp(jnp.log(jnp.abs(code)) * (1.0 / POWER)) * (1.0 / CODE_SCALE)
    return jnp.where(code < 0, -size, size)


def shape(rows, width, dtype=F32):
    return jax.ShapeDtypeStruct((rows, width), dtype)


def block(rows, width, row=0, column=0):
    return pl.BlockSpec((rows, width), lambda *_: (row, column))


class Line:
    def __init__(self):
        self.token = None
        self.extra = []

    def after(self, *arrays):
        self.extra += arrays

    def run(self, kernel, inputs, in_specs, outs, out_specs, grid=(1,), scalars=(), limit=24, flops=0):
        inputs, in_specs = list(inputs), list(in_specs)
        size = sum(math.prod(a.shape) * jnp.dtype(a.dtype).itemsize for a in (*inputs, *outs))
        waits = [*self.extra, *([] if self.token is None else [self.token])]
        self.extra, skip = [], len(waits)
        inputs += waits
        in_specs += [pl.BlockSpec(memory_space=pl.ANY)] * skip
        given = len(scalars) + len(inputs)

        def body(*refs):
            kernel(*refs[: given - skip], *refs[given:-1])
            refs[-1][...] = jnp.zeros((8, 128), F32)

        result = pl.pallas_call(
            body,
            grid_spec=pltpu.PrefetchScalarGridSpec(
                num_scalar_prefetch=len(scalars),
                grid=grid,
                in_specs=in_specs,
                out_specs=[*out_specs, block(8, 128)],
            ),
            out_shape=[*outs, shape(8, 128)],
            cost_estimate=pl.CostEstimate(
                flops=int(COST_SHARE * flops), bytes_accessed=int(COST_SHARE * size), transcendentals=0
            ),
            compiler_params=pltpu.CompilerParams(vmem_limit_bytes=limit * 2**20),
        )(*scalars, *inputs)
        *result, self.token = result
        return result[0] if len(outs) == 1 else result


def copy_kernel(in_ref, out_ref):
    out_ref[...] = in_ref[...]


def columns(line, matrix, start, width, limit=24):
    rows = matrix.shape[0]
    tile = 256
    return line.run(
        copy_kernel,
        (matrix,),
        (pl.BlockSpec((rows, tile), lambda n: (0, start // tile + n)),),
        (shape(rows, width, matrix.dtype),),
        (pl.BlockSpec((rows, tile), lambda n: (0, n)),),
        grid=(width // tile,),
        limit=limit,
    )


def pack_kernel(place_ref, near_ref, far_ref, out_ref):
    rows = near_ref.shape[1]
    out_ref[:rows, :] = near_ref[...].T
    out_ref[rows:, :] = far_ref[...].T


def pack(line, context, place, rows):
    tokens, width = context.shape

    def column(half, step, place):
        core, x, y = place[0], place[1], place[2]
        turn = jnp.where(core == 0, 2 * X - 1 - step, 1 + step)
        return (0, ((y + half) % HALVES) * (2 * X) + ((x + turn) % X) * 2 + core)

    return line.run(
        pack_kernel,
        (context, context),
        (
            pl.BlockSpec((tokens, rows), functools.partial(column, 0)),
            pl.BlockSpec((tokens, rows), functools.partial(column, 1)),
        ),
        (shape(width // 2, tokens, context.dtype),),
        (pl.BlockSpec((2 * rows, tokens), lambda step, place: (step, 0)),),
        grid=(X,),
        scalars=(place,),
    )


def both(own_lhs, other_lhs, own_rhs, other_rhs):
    total = jnp.dot(own_lhs[...], own_rhs[...], preferred_element_type=F32)
    return total + jnp.dot(other_lhs[...], other_rhs[...], preferred_element_type=F32)


def first_kernel(own_lhs, other_lhs, own_rhs, other_rhs, code_ref):
    code_ref[...] = encode(both(own_lhs, other_lhs, own_rhs, other_rhs))


def relay_kernel(own_lhs, other_lhs, own_rhs, other_rhs, arrived_ref, code_ref):
    code_ref[...] = encode(both(own_lhs, other_lhs, own_rhs, other_rhs) + decode(arrived_ref[...]))


def settle_kernel(own_lhs, other_lhs, own_rhs, other_rhs, arrived_ref, keep_ref, code_ref):
    total = both(own_lhs, other_lhs, own_rhs, other_rhs) + decode(arrived_ref[...])
    rows = keep_ref.shape[0]
    keep_ref[...] = total[:rows]
    code_ref[...] = encode(total[rows:])


def crossed_kernel(own_lhs, other_lhs, own_rhs, other_rhs, code_ref, out_ref):
    total = both(own_lhs, other_lhs, own_rhs, other_rhs)
    rows = total.shape[0] // (2 * X)
    for s in range(X):
        out_ref[s * rows : (s + 1) * rows, :] = total[2 * s * rows : (2 * s + 1) * rows]
        code_ref[s * rows : (s + 1) * rows, :] = encode(total[(2 * s + 1) * rows : (2 * s + 2) * rows])


def product(line, kernel, lhs, own_cot, other_cot, start, step, rows, outs, arrived=None):
    tokens, width = other_cot.shape
    lhs_spec = block(rows, tokens, step)
    inputs = [*lhs, own_cot, other_cot]
    specs = [
        lhs_spec,
        lhs_spec,
        pl.BlockSpec((tokens, TILE), lambda n: (0, start // TILE + n)),
        pl.BlockSpec((tokens, TILE), lambda n: (0, n)),
    ]
    if arrived is not None:
        inputs.append(arrived)
        specs.append(pl.BlockSpec((rows, TILE), lambda n: (0, n)))
    return line.run(
        kernel,
        inputs,
        specs,
        [shape(r, width, t) for r, t in outs],
        [pl.BlockSpec((r, TILE), lambda n: (0, n)) for r, _ in outs],
        grid=(width // TILE,),
        limit=28,
        flops=4 * rows * tokens * width,
    )


def spread_kernel(own_ref, crossed_ref, *out_refs):
    rows = out_refs[0].shape[0]
    for s, out_ref in enumerate(out_refs):
        part = slice(s * rows, (s + 1) * rows)
        total = own_ref[part, :] + decode(crossed_ref[part, :])
        out_ref[...] = encode(total) if s < X - 1 else total


def spread(line, own, crossed):
    width = own.shape[1]
    rows = own.shape[0] // X
    whole = block(X * rows, width)
    return line.run(
        spread_kernel,
        (own, crossed),
        (whole, whole),
        [shape(rows, width, BF16)] * (X - 1) + [shape(rows, width)],
        [block(rows, width)] * X,
        limit=16,
    )


def three(value):
    high = value.astype(BF16).astype(F32)
    rest = value - high
    middle = rest.astype(BF16).astype(F32)
    low = rest - middle
    return jnp.concatenate([high, middle, low, jnp.zeros_like(low)], axis=0).astype(BF16)


def added(parts):
    rows = parts.shape[0] // 4
    return parts[:rows] + (parts[rows : 2 * rows] + parts[2 * rows : 3 * rows])


def project_kernel(right_ref, left_ref, weights_ref, own_right, own_left):
    rank = right_ref.shape[0]
    vectors = three(jnp.concatenate([right_ref[...], left_ref[...]], axis=0))
    both_edges = added(lax.dot_general(vectors, weights_ref[...], LAST, preferred_element_type=F32))
    own_right[...] = both_edges[:rank]
    own_left[...] = both_edges[rank:]


def project(line, right, left, weights):
    rank, width = right.shape
    rows = weights.shape[0]
    return line.run(
        project_kernel,
        (right, left, weights),
        (block(rank, width), block(rank, width), block(rows, width)),
        (shape(rank, rows), shape(rank, rows)),
        (block(rank, rows), block(rank, rows)),
    )


def edge_kernel(own_right, own_left, from_right, from_left, weights_ref, sums_ref, left_ref, lowrank_ref):
    right = own_right[...] - from_right[...]
    left = from_left[...] - own_left[...]
    rank, rows = right.shape
    width = weights_ref.shape[1]
    lowrank_ref[...] = right
    both_edges = three(jnp.concatenate([right, left], axis=0))
    both_edges = added(jnp.dot(both_edges, weights_ref[...], preferred_element_type=F32))
    sums_ref[:, :width] = both_edges[:rank]
    left_ref[...] = both_edges[rank:]
    square = jnp.concatenate([right, jnp.zeros((128 - rank, rows), F32)], axis=0)
    sums_ref[:, width:] = lax.dot_general(right, square, LAST, precision=HIGH, preferred_element_type=F32)


def edge_sums(line, own_right, own_left, from_right, from_left, weights):
    rank, rows = own_right.shape
    width = weights.shape[1]
    small = block(rank, rows)
    return line.run(
        edge_kernel,
        (own_right, own_left, from_right, from_left, weights),
        (small, small, small, small, block(rows, width)),
        (shape(rank, width + 128), shape(rank, width), shape(rank, rows)),
        (block(rank, width + 128), block(rank, width), small),
    )


def less_kernel(one_ref, two_ref, out_ref):
    width = two_ref.shape[1]
    out_ref[:, :width] = one_ref[:, :width] - two_ref[...]
    out_ref[:, width:] = one_ref[:, width:]


def plus_kernel(one_ref, two_ref, out_ref):
    out_ref[...] = one_ref[...] + two_ref[...]


def plus_ring_kernel(own_ref, one_ref, two_ref, three_ref, out_ref):
    out_ref[...] = (own_ref[...] + two_ref[...]) + (one_ref[...] + three_ref[...])


def combine(line, kernel, *arrays):
    return line.run(
        kernel,
        arrays,
        [block(*array.shape) for array in arrays],
        (shape(*arrays[0].shape),),
        (block(*arrays[0].shape),),
        limit=16,
    )


def solve_kernel(one_ref, two_ref, lowrank_ref, vectors_ref, packed_ref):
    rank = lowrank_ref.shape[0]
    width = vectors_ref.shape[1]
    gram = one_ref[:, width:] + two_ref[:, width:]
    right = one_ref[:, :width] + two_ref[:, :width]
    lowrank = lowrank_ref[...]
    row = lax.broadcasted_iota(jnp.int32, (rank, 1), 0)

    def step(matrix, k, factor, inverse):
        pivot = matrix[k : k + 1, :] * inverse
        return jnp.where(row == k, pivot, matrix - factor * pivot)

    for k in range(rank):
        inverse = 1.0 / jnp.sqrt(gram[k : k + 1, k : k + 1])
        factor = jnp.where(row > k, gram[:, k : k + 1] * inverse, 0.0)
        gram, right, lowrank = (step(m, k, factor, inverse) for m in (gram, right, lowrank))
    vectors_ref[...] = right
    packed_ref[:, :width] = right
    packed_ref[:, width:] = lowrank


def solve(line, one, two, lowrank):
    rank, rows = lowrank.shape
    width = one.shape[1] - 128
    return line.run(
        solve_kernel,
        (one, two, lowrank),
        (block(*one.shape), block(*one.shape), block(rank, rows)),
        (shape(rank, width), shape(rank, width + rows)),
        (block(rank, width), block(rank, width + rows)),
        limit=16,
    )


def mix_kernel(weights_ref, right_ref, left_ref, right_basis, left_basis, out_ref):
    def parts(value):
        high = value.astype(BF16)
        rest = value - high.astype(F32)
        middle = rest.astype(BF16)
        return high, middle, (rest - middle.astype(F32)).astype(BF16)

    b = parts(jnp.concatenate([right_basis[...], -left_basis[...]], axis=0))
    v = parts(jnp.concatenate([right_ref[...], left_ref[...]], axis=0))
    pairs = ((0, 0), (0, 1), (1, 0), (0, 2), (2, 0), (1, 1))
    approx = lax.dot_general(
        jnp.concatenate([b[i] for i, _ in pairs], axis=0),
        jnp.concatenate([v[j] for _, j in pairs], axis=0),
        (((0,), (0,)), ((), ())),
        preferred_element_type=F32,
    )
    out_ref[...] = weights_ref[...].astype(F32) - gossip_rate * approx


def mix(line, weights, right, left):
    rows, width = weights.shape
    rank = right.shape[0]
    tile = 1024
    vectors = pl.BlockSpec((rank, tile), lambda n: (0, n))
    basis = block(rank, rows, 0, width // rows)
    wide = pl.BlockSpec((rows, tile), lambda n: (0, n))
    return line.run(
        mix_kernel,
        (weights, right, left, right, left),
        (wide, vectors, vectors, basis, basis),
        (shape(rows, width),),
        (wide,),
        grid=(width // tile,),
        limit=16,
    )


def finish_kernel(rate, parts, mixed_ref, *refs):
    out_ref = refs[-1]
    start = used = 0
    for count in parts:
        total = refs[used][...]
        for code in refs[used + 1 : used + count]:
            total += decode(code[...])
        part = slice(start, start + total.shape[1])
        out_ref[:, part] = mixed_ref[:, part] - rate * total
        start, used = part.stop, used + count


def finish(line, rate, mixed, parts):
    flat = [array for group in parts for array in group]
    whole = block(*mixed.shape)
    return line.run(
        functools.partial(finish_kernel, rate, [len(group) for group in parts]),
        (mixed, *flat),
        (whole, *[block(*array.shape) for array in flat]),
        (shape(*mixed.shape),),
        (whole,),
        limit=20,
    )


def local(context, cotangent, weights, edge_vectors):
    groups = lax.axis_size("fsdp")
    replicas = lax.axis_size("blk")
    context, cotangent, weights, edge = context[0], cotangent[0], weights[0], edge_vectors[0]
    tokens, width = cotangent.shape
    rows = weights.shape[0]
    pair = HALVES * rows
    b_width = a_width = 3 * width // 8
    a_start, c_start = b_width, b_width + a_width
    c_width = width - c_start

    place = lax.axis_index("fsdp")
    core, x, y = place % 2, (place // 2) % X, place // (2 * X)
    own_place = jnp.stack([core, x, y]).astype(jnp.int32)
    other_place = jnp.stack([1 - core, x, y]).astype(jnp.int32)

    def move(value, target):
        return lax.ppermute(value, "fsdp", [(i, target(i)) for i in range(groups)])

    def flip(bit):
        return lambda i: i ^ bit

    other_core, other_half = flip(1), flip(2 * X)

    def along(by):
        def target(i):
            ahead = by if i % 2 == 0 else X - by
            return i // (2 * X) * (2 * X) + ((i // 2 + ahead) % X) * 2 + i % 2

        return target

    def turn(value, by):
        return lax.ppermute(value, "blk", [(i, (i + by) % replicas) for i in range(replicas)])

    line = Line()

    left_edge = turn(edge, 1)
    packed = pack(line, context, other_place, rows)
    other_lhs = move(packed, other_core)
    b_cot = columns(line, cotangent, 0, b_width)
    b_other = move(b_cot, other_core)
    a_cot = columns(line, cotangent, a_start, a_width)
    a_other = move(a_cot, other_core)
    own_lhs = pack(line, context, own_place, rows)
    line.after(left_edge)
    c_cot = columns(line, cotangent, c_start, c_width)
    c_other = move(c_cot, other_core)
    times = functools.partial(product, line, lhs=(own_lhs, other_lhs), own_cot=cotangent)
    b_part = dict(other_cot=b_other, start=0, rows=pair)
    a_part = dict(other_cot=a_other, start=a_start, rows=pair)
    whole = [(pair, BF16)]
    halves = [(rows, F32), (rows, BF16)]

    b1 = move(times(first_kernel, **b_part, step=0, outs=whole), along(1))
    a1 = move(times(first_kernel, **a_part, step=0, outs=whole), along(1))
    own_right, own_left = project(line, edge, left_edge, weights)
    from_left = turn(own_right, 1)
    from_right = turn(own_left, -1)
    c_code, c_own = times(
        crossed_kernel,
        other_cot=c_other,
        start=c_start,
        step=0,
        rows=X * pair,
        outs=[(X * rows, BF16), (X * rows, F32)],
    )
    c_cross = move(c_code, other_half)
    sums, sums_left, lowrank = edge_sums(line, own_right, own_left, from_right, from_left, weights)
    sums_right = turn(sums_left, -1)
    b2 = move(times(relay_kernel, **b_part, step=1, outs=whole, arrived=b1), along(1))
    sums = combine(line, less_kernel, sums, sums_right)
    sums_other = move(sums, other_core)
    a2 = move(times(relay_kernel, **a_part, step=1, outs=whole, arrived=a1), along(1))
    sums = combine(line, plus_kernel, sums, sums_other)
    sums_other = [move(sums, flip(2 * by)) for by in (1, 2, 3)]
    b3 = move(times(relay_kernel, **b_part, step=2, outs=whole, arrived=b2), along(1))
    sums = combine(line, plus_ring_kernel, sums, *sums_other)
    sums_other = move(sums, other_half)
    a3 = move(times(relay_kernel, **a_part, step=2, outs=whole, arrived=a2), along(1))
    new_vectors, right = solve(line, sums, sums_other, lowrank)
    left = turn(right, 1)
    b_keep, b_send = times(settle_kernel, **b_part, step=3, outs=halves, arrived=b3)
    b_cross = move(b_send, other_half)
    *c_codes, c_keep = spread(line, c_own, c_cross)
    c_codes = [move(code, along(X - 1 - s)) for s, code in enumerate(c_codes)]
    mixed = mix(line, weights, right, left)
    a_keep, a_send = times(settle_kernel, **a_part, step=3, outs=halves, arrived=a3)
    a_cross = move(a_send, other_half)
    rate = learn_rate / math.sqrt(groups * tokens)
    new_weights = finish(
        line, rate, mixed, [(b_keep, b_cross), (a_keep, a_cross), (c_keep, *c_codes)]
    )
    return (new_weights[None], new_vectors[None])


def solution(mesh):
    return jax.shard_map(
        local,
        mesh=mesh,
        in_specs=(
            P("blk", "fsdp", None),
            P("blk", "fsdp", None),
            P("blk", "fsdp", None),
            P("blk", None, None),
        ),
        out_specs=(P("blk", "fsdp", None), P("blk", None, None)),
        check_vma=False,
    )
```

```python
import functools
import math

import jax
import jax.numpy as jnp
from jax import lax
from jax.experimental import pallas as pl
from jax.experimental.pallas import tpu as pltpu
from jax.sharding import PartitionSpec as P

learn_rate = 0.5
gossip_rate = 0.5

X = 4
HALVES = 2
TILE = 512
POWER = 9
TINY = 1e-37
CODE_SCALE = 2.0**-5

ORDER = ("a0", "c", "b1", "a1", "edge", "b2", "add", "a2", "sum_x", "b3", "solve", "c0", "c1", "a3", "mix", "c2")
HIGH = lax.Precision.HIGHEST
SHARES = dict(pack1=1.0, pack2=1.0, b0=30.0, a0=1.0, c=1.0, b1=3.0, b2=3.0)
WIDTHS = (1536, 1536)
F32 = jnp.float32
BF16 = jnp.bfloat16
LAST = (((1,), (1,)), ((), ()))


def encode(total):
    z = total * CODE_SCALE
    z2 = z * z
    z4 = z2 * z2
    return (z4 * z4 * z).astype(BF16)


def decode(code):
    code = code.astype(F32)
    size = jnp.log(jnp.maximum(jnp.abs(code), TINY))
    return code * lax.exp2(size * ((1.0 / POWER - 1.0) / math.log(2.0)) - math.log2(CODE_SCALE))


def shape(rows, width, dtype=F32):
    return jax.ShapeDtypeStruct((rows, width), dtype)


def block(rows, width, row=0, column=0):
    return pl.BlockSpec((rows, width), lambda *_: (row, column))


class Line:
    def __init__(self):
        self.token = None
        self.name = None

    def run(self, kernel, inputs, in_specs, outs, out_specs, grid=(1,), scalars=(), limit=24, flops=0):
        share = SHARES.get(self.name, 10.0)
        inputs, in_specs = list(inputs), list(in_specs)
        size = sum(math.prod(a.shape) * jnp.dtype(a.dtype).itemsize for a in (*inputs, *outs))
        waits = [] if self.token is None else [self.token]
        skip = len(waits)
        inputs += waits
        in_specs += [pl.BlockSpec(memory_space=pl.ANY)] * skip
        given = len(scalars) + len(inputs)

        def body(*refs):
            kernel(*refs[: given - skip], *refs[given:-1])
            refs[-1][...] = jnp.zeros((8, 128), F32)

        result = pl.pallas_call(
            body,
            grid_spec=pltpu.PrefetchScalarGridSpec(
                num_scalar_prefetch=len(scalars),
                grid=grid,
                in_specs=in_specs,
                out_specs=[*out_specs, block(8, 128)],
            ),
            out_shape=[*outs, shape(8, 128)],
            cost_estimate=pl.CostEstimate(
                flops=int(share * flops), bytes_accessed=int(share * size), transcendentals=0
            ),
            compiler_params=pltpu.CompilerParams(vmem_limit_bytes=limit * 2**20),
        )(*scalars, *inputs)
        *result, self.token = result
        return result[0] if len(outs) == 1 else result


def pack_kernel(count, place_ref, near_ref, far_ref, *refs):
    out_ref = refs[count]
    rows = near_ref.shape[1]
    out_ref[:rows, :] = near_ref[...].T
    out_ref[rows:, :] = far_ref[...].T
    for part_ref, copy_ref in zip(refs[:count], refs[count + 1 :]):
        copy_ref[...] = part_ref[...]


def pack(line, context, place, rows, cotangent, parts, limit=24):
    tokens, width = context.shape

    def column(half, step, place):
        core, x, y = place[0], place[1], place[2]
        turn = jnp.where(core == 0, 2 * X - 1 - step, 1 + step)
        return (0, ((y + half) % HALVES) * (2 * X) + ((x + turn) % X) * 2 + core)

    def taken(start, size):
        tile = size // X
        return pl.BlockSpec((tokens, tile), lambda step, place: (0, start // tile + step))

    return line.run(
        functools.partial(pack_kernel, len(parts)),
        (context, context, *[cotangent] * len(parts)),
        (
            pl.BlockSpec((tokens, rows), functools.partial(column, 0)),
            pl.BlockSpec((tokens, rows), functools.partial(column, 1)),
            *[taken(*part) for part in parts],
        ),
        (shape(width // 2, tokens, BF16), *[shape(tokens, size, BF16) for _, size in parts]),
        (
            pl.BlockSpec((2 * rows, tokens), lambda step, place: (step, 0)),
            *[taken(0, size) for _, size in parts],
        ),
        grid=(X,),
        scalars=(place,),
        limit=limit,
    )


def both(own_lhs, other_lhs, own_rhs, other_rhs, part=slice(None)):
    total = jnp.dot(own_lhs[...], own_rhs[:, part], preferred_element_type=F32)
    return total + jnp.dot(other_lhs[...], other_rhs[:, part], preferred_element_type=F32)


def parts_of(ref):
    width = ref.shape[1]
    return [slice(start, start + 256) for start in range(0, width, 256)]


def first_kernel(own_lhs, other_lhs, own_rhs, other_rhs, code_ref):
    for part in parts_of(code_ref):
        code_ref[:, part] = encode(both(own_lhs, other_lhs, own_rhs, other_rhs, part))


def relay_kernel(own_lhs, other_lhs, own_rhs, other_rhs, arrived_ref, code_ref):
    for part in parts_of(code_ref):
        total = both(own_lhs, other_lhs, own_rhs, other_rhs, part) + decode(arrived_ref[:, part])
        code_ref[:, part] = encode(total)


def settle_kernel(own_lhs, other_lhs, own_rhs, other_rhs, arrived_ref, keep_ref, code_ref):
    rows = keep_ref.shape[0]
    for part in parts_of(code_ref):
        total = both(own_lhs, other_lhs, own_rhs, other_rhs, part) + decode(arrived_ref[:, part])
        keep_ref[:, part] = total[:rows]
        code_ref[:, part] = encode(total[rows:])


def crossed_kernel(own_lhs, other_lhs, own_rhs, other_rhs, code_ref, out_ref):
    total = both(own_lhs, other_lhs, own_rhs, other_rhs)
    rows = total.shape[0] // (2 * X)
    for s in range(X):
        out_ref[s * rows : (s + 1) * rows, :] = total[2 * s * rows : (2 * s + 1) * rows]
        code_ref[s * rows : (s + 1) * rows, :] = encode(total[(2 * s + 1) * rows : (2 * s + 2) * rows])


def product(line, kernel, lhs, own_cot, other_cot, start, step, rows, outs, arrived=None):
    tokens, width = other_cot.shape
    lhs_spec = block(rows, tokens, step)
    inputs = [*lhs, own_cot, other_cot]
    specs = [
        lhs_spec,
        lhs_spec,
        pl.BlockSpec((tokens, TILE), lambda n: (0, start // TILE + n)),
        pl.BlockSpec((tokens, TILE), lambda n: (0, n)),
    ]
    if arrived is not None:
        inputs.append(arrived)
        specs.append(pl.BlockSpec((rows, TILE), lambda n: (0, n)))
    return line.run(
        kernel,
        inputs,
        specs,
        [shape(r, width, t) for r, t in outs],
        [pl.BlockSpec((r, TILE), lambda n: (0, n)) for r, _ in outs],
        grid=(width // TILE,),
        limit=28,
        flops=4 * rows * tokens * width,
    )


def open_kernel(own_ref, crossed_ref, out_ref):
    out_ref[...] = encode(own_ref[...] + decode(crossed_ref[...]))


def pass_kernel(own_ref, crossed_ref, arrived_ref, out_ref):
    out_ref[...] = encode(own_ref[...] + decode(crossed_ref[...]) + decode(arrived_ref[...]))


def pass_on(line, own, crossed, step, arrived=None):
    width = own.shape[1]
    rows = own.shape[0] // X
    here = block(rows, width, step)
    arrived = [] if arrived is None else [arrived]
    return line.run(
        pass_kernel if arrived else open_kernel,
        (own, crossed, *arrived),
        (here, here, *[block(rows, width)] * len(arrived)),
        (shape(rows, width, BF16),),
        (block(rows, width),),
        limit=16,
    )


def three(value):
    high = value.astype(BF16).astype(F32)
    rest = value - high
    middle = rest.astype(BF16).astype(F32)
    low = rest - middle
    return jnp.concatenate([high, middle, low, jnp.zeros_like(low)], axis=0).astype(BF16)


def added(parts):
    rows = parts.shape[0] // 4
    return parts[:rows] + (parts[rows : 2 * rows] + parts[2 * rows : 3 * rows])


def edge_kernel(own_ref, next_ref, edge_ref, sums_ref, lowrank_ref):
    differ = own_ref[...].astype(F32) - next_ref[...].astype(F32)
    high = differ.astype(BF16)
    low = (differ - high.astype(F32)).astype(BF16)

    def times(rows, axes):
        parts = three(rows)
        return added(
            lax.dot_general(parts, high, axes, preferred_element_type=F32)
            + lax.dot_general(parts, low, axes, preferred_element_type=F32)
        )

    lowrank = times(edge_ref[...], LAST)
    lowrank_ref[...] = lowrank
    width = differ.shape[1]
    sums_ref[:, :width] = times(lowrank, (((1,), (0,)), ((), ())))
    rank, rows = lowrank.shape
    square = jnp.concatenate([lowrank, jnp.zeros((128 - rank, rows), F32)], axis=0)
    sums_ref[:, width:] = lax.dot_general(lowrank, square, LAST, precision=HIGH, preferred_element_type=F32)


def edge_sums(line, own, following, edge):
    rows, width = own.shape
    rank = edge.shape[0]
    return line.run(
        edge_kernel,
        (own, following, edge),
        (block(rows, width), block(rows, width), block(rank, width)),
        (shape(rank, width + 128), shape(rank, rows)),
        (block(rank, width + 128), block(rank, rows)),
    )


def plus_kernel(one_ref, two_ref, out_ref):
    out_ref[...] = one_ref[...] + two_ref[...]


def plus_ring_kernel(own_ref, one_ref, two_ref, three_ref, out_ref):
    out_ref[...] = (own_ref[...] + two_ref[...]) + (one_ref[...] + three_ref[...])


def combine(line, kernel, *arrays):
    return line.run(
        kernel,
        arrays,
        [block(*array.shape) for array in arrays],
        (shape(*arrays[0].shape),),
        (block(*arrays[0].shape),),
        limit=16,
    )


def solve_kernel(one_ref, two_ref, lowrank_ref, vectors_ref, packed_ref):
    rank = lowrank_ref.shape[0]
    width = vectors_ref.shape[1]
    gram = one_ref[:, width:] + two_ref[:, width:]
    right = one_ref[:, :width] + two_ref[:, :width]
    lowrank = lowrank_ref[...]
    row = lax.broadcasted_iota(jnp.int32, (rank, 1), 0)

    def step(matrix, k, factor, inverse):
        pivot = matrix[k : k + 1, :] * inverse
        return jnp.where(row == k, pivot, matrix - factor * pivot)

    for k in range(rank):
        inverse = 1.0 / jnp.sqrt(gram[k : k + 1, k : k + 1])
        factor = jnp.where(row > k, gram[:, k : k + 1] * inverse, 0.0)
        gram, right, lowrank = (step(m, k, factor, inverse) for m in (gram, right, lowrank))
    vectors_ref[...] = right
    packed_ref[:, :width] = right
    packed_ref[:, width:] = lowrank


def solve(line, one, two, lowrank):
    rank, rows = lowrank.shape
    width = one.shape[1] - 128
    return line.run(
        solve_kernel,
        (one, two, lowrank),
        (block(*one.shape), block(*one.shape), block(rank, rows)),
        (shape(rank, width), shape(rank, width + rows)),
        (block(rank, width), block(rank, width + rows)),
        limit=16,
    )


def mix_kernel(rate, weights_ref, right_ref, left_ref, right_basis, left_basis, keep_ref, code_ref, out_ref):
    def parts(value):
        high = value.astype(BF16)
        rest = value - high.astype(F32)
        middle = rest.astype(BF16)
        return high, middle, (rest - middle.astype(F32)).astype(BF16)

    b = parts(jnp.concatenate([right_basis[...], -left_basis[...]], axis=0))
    v = parts(jnp.concatenate([right_ref[...], left_ref[...]], axis=0))
    pairs = ((0, 0), (0, 1), (1, 0), (0, 2), (2, 0), (1, 1))
    approx = lax.dot_general(
        jnp.concatenate([b[i] for i, _ in pairs], axis=0),
        jnp.concatenate([v[j] for _, j in pairs], axis=0),
        (((0,), (0,)), ((), ())),
        preferred_element_type=F32,
    )
    mixed = weights_ref[...].astype(F32) - gossip_rate * approx
    width = keep_ref.shape[1]
    out_ref[:, :width] = mixed[:, :width] - rate * (keep_ref[...] + decode(code_ref[...]))
    out_ref[:, width:] = mixed[:, width:]


def mix(line, rate, weights, right, left, keep, code):
    rows, width = weights.shape
    rank = right.shape[0]
    vectors, whole = block(rank, width), block(rows, width)
    basis = block(rank, rows, 0, width // rows)
    return line.run(
        functools.partial(mix_kernel, rate),
        (weights, right, left, right, left, keep, code),
        (whole, vectors, vectors, basis, basis, block(*keep.shape), block(*code.shape)),
        (shape(rows, width),),
        (whole,),
        limit=20,
    )


def finish_kernel(rate, start, counts, mixed_ref, *refs):
    out_ref = refs[-1]
    out_ref[:, :start] = mixed_ref[:, :start]
    used = 0
    for count in counts:
        total = refs[used][...]
        for code in refs[used + 1 : used + count]:
            total += decode(code[...])
        part = slice(start, start + total.shape[1])
        out_ref[:, part] = mixed_ref[:, part] - rate * total
        start, used = part.stop, used + count


def finish(line, rate, start, mixed, parts):
    rows = mixed.shape[0]
    flat = [array for group in parts for array in group]
    whole = block(*mixed.shape)
    return line.run(
        functools.partial(finish_kernel, rate, start, [len(group) for group in parts]),
        (mixed, *flat),
        (whole, *[block(rows, array.shape[1], array.shape[0] // rows - 1) for array in flat]),
        (shape(*mixed.shape),),
        (whole,),
        limit=20,
    )


def local(context, cotangent, weights, edge_vectors):
    groups = lax.axis_size("fsdp")
    replicas = lax.axis_size("blk")
    context, cotangent, weights, edge = context[0], cotangent[0], weights[0], edge_vectors[0]
    tokens, width = cotangent.shape
    rows = weights.shape[0]
    pair = HALVES * rows
    b_width, a_width = WIDTHS
    a_start, c_start = b_width, b_width + a_width
    c_width = width - c_start

    place = lax.axis_index("fsdp")
    core, x, y = place % 2, (place // 2) % X, place // (2 * X)
    own_place = jnp.stack([core, x, y]).astype(jnp.int32)
    other_place = jnp.stack([1 - core, x, y]).astype(jnp.int32)

    def move(value, target):
        return lax.ppermute(value, "fsdp", [(i, target(i)) for i in range(groups)])

    def flip(bit):
        return lambda i: i ^ bit

    other_core, other_half = flip(1), flip(2 * X)

    def along(by):
        def target(i):
            ahead = by if i % 2 == 0 else X - by
            return i // (2 * X) * (2 * X) + ((i // 2 + ahead) % X) * 2 + i % 2

        return target

    def turn(value, by):
        return lax.ppermute(value, "blk", [(i, (i + by) % replicas) for i in range(replicas)])

    line = Line()

    line.name = "pack1"
    other_lhs, b_cot = pack(line, context, other_place, rows, cotangent, [(0, b_width)])
    other_lhs, b_other = move(other_lhs, other_core), move(b_cot, other_core)
    line.name = "pack2"
    parts = [(a_start, a_width), (c_start, c_width)]
    own_lhs, a_cot, c_cot = pack(line, context, own_place, rows, cotangent, parts, 24)
    a_other, c_other = move(a_cot, other_core), move(c_cot, other_core)
    times = functools.partial(product, line, lhs=(own_lhs, other_lhs), own_cot=cotangent)
    b_part = dict(other_cot=b_other, start=0, rows=pair)
    a_part = dict(other_cot=a_other, start=a_start, rows=pair)
    whole = [(pair, BF16)]
    halves = [(rows, F32), (rows, BF16)]

    line.name = "b0"
    following = turn(weights, -1)
    b1 = move(times(first_kernel, **b_part, step=0, outs=whole), along(1))
    rate = learn_rate / math.sqrt(groups * tokens)
    have = {"b1": b1}

    def step_a0():
        have["a1"] = move(times(first_kernel, **a_part, step=0, outs=whole), along(1))

    def step_c():
        outs = [(X * rows, BF16), (X * rows, F32)]
        part = dict(other_cot=c_other, start=c_start, step=0, rows=X * pair)
        code, have["c_own"] = times(crossed_kernel, **part, outs=outs)
        have["c_cross"] = move(code, other_half)

    def step_edge():
        have["sums"], have["lowrank"] = edge_sums(line, weights, following, edge)
        have["sums_core"] = move(have["sums"], other_core)

    def step_add():
        have["sums"] = combine(line, plus_kernel, have["sums"], have["sums_core"])
        have["sums_x"] = [move(have["sums"], flip(2 * by)) for by in (1, 2, 3)]

    def step_sum_x():
        have["sums"] = combine(line, plus_ring_kernel, have["sums"], *have["sums_x"])
        have["sums_y"] = move(have["sums"], other_half)

    def step_solve():
        have["vectors"], have["right"] = solve(line, have["sums"], have["sums_y"], have["lowrank"])
        have["left"] = turn(have["right"], 1)

    def step_mix():
        have["mixed"] = mix(line, rate, weights, have["right"], have["left"], *have["b_last"])

    def step_ring(name, part, step):
        before, after = f"{name}{step}", f"{name}{step + 1}"
        code = times(relay_kernel, **part, step=step, outs=whole, arrived=have[before])
        have[after] = move(code, along(1))

    def step_settle(name, part):
        keep, send = times(settle_kernel, **part, step=X - 1, outs=halves, arrived=have[f"{name}{X - 1}"])
        have[f"{name}_last"] = keep, move(send, other_half)

    def step_pass(step):
        code = pass_on(line, have["c_own"], have["c_cross"], step, have.get(f"c{step}"))
        have[f"c{step + 1}"] = move(code, along(1))

    steps = dict(
        a0=step_a0,
        c=step_c,
        edge=step_edge,
        add=step_add,
        sum_x=step_sum_x,
        solve=step_solve,
        mix=step_mix,
        b1=lambda: step_ring("b", b_part, 1),
        b2=lambda: step_ring("b", b_part, 2),
        b3=lambda: step_settle("b", b_part),
        a1=lambda: step_ring("a", a_part, 1),
        a2=lambda: step_ring("a", a_part, 2),
        a3=lambda: step_settle("a", a_part),
        c0=lambda: step_pass(0),
        c1=lambda: step_pass(1),
        c2=lambda: step_pass(2),
    )
    for name in ORDER:
        line.name = name
        steps[name]()
    line.name = "finish"
    last = have["c_own"], have["c_cross"], have["c3"]
    new_weights, new_vectors = finish(line, rate, a_start, have["mixed"], [have["a_last"], last]), have["vectors"]
    return (new_weights[None], new_vectors[None])


def solution(mesh):
    return jax.shard_map(
        local,
        mesh=mesh,
        in_specs=(
            P("blk", "fsdp", None),
            P("blk", "fsdp", None),
            P("blk", "fsdp", None),
            P("blk", None, None),
        ),
        out_specs=(P("blk", "fsdp", None), P("blk", None, None)),
        check_vma=False,
    )
```

```python
import functools
import math

import jax
import jax.numpy as jnp
from jax import lax
from jax.experimental import pallas as pl
from jax.experimental.pallas import tpu as pltpu
from jax.sharding import PartitionSpec as P

learn_rate = 0.5
gossip_rate = 0.5

X = 4
HALVES = 2
TILE = 512
POWER = 9
TINY = 1e-37
CODE_SCALE = 2.0**-5

ORDER = ("a0", "c", "b1", "a1", "edge", "b2", "add", "a2", "sum_x", "b3", "c0", "solve", "a3", "c1", "mix", "c2")
HIGH = lax.Precision.HIGHEST
SHARES = dict(pack1=1.0, slice=1.0, pack2=1.0, b0=30.0, a0=1.0, c=1.0, b1=3.0, b2=3.0)
WIDTHS = (1536, 1536)
F32 = jnp.float32
BF16 = jnp.bfloat16
LAST = (((1,), (1,)), ((), ()))


def encode(total):
    z = total * CODE_SCALE
    z2 = z * z
    z4 = z2 * z2
    return (z4 * z4 * z).astype(BF16)


def decode(code):
    code = code.astype(F32)
    size = jnp.log(jnp.maximum(jnp.abs(code), TINY))
    return code * lax.exp2(size * ((1.0 / POWER - 1.0) / math.log(2.0)) - math.log2(CODE_SCALE))


def shape(rows, width, dtype=F32):
    return jax.ShapeDtypeStruct((rows, width), dtype)


def block(rows, width, row=0, column=0):
    return pl.BlockSpec((rows, width), lambda *_: (row, column))


class Line:
    def __init__(self):
        self.token = None
        self.name = None

    def run(self, kernel, inputs, in_specs, outs, out_specs, grid=(1,), scalars=(), limit=24, flops=0):
        share = SHARES.get(self.name, 10.0)
        inputs, in_specs = list(inputs), list(in_specs)
        size = sum(math.prod(a.shape) * jnp.dtype(a.dtype).itemsize for a in (*inputs, *outs))
        waits = [] if self.token is None else [self.token]
        skip = len(waits)
        inputs += waits
        in_specs += [pl.BlockSpec(memory_space=pl.ANY)] * skip
        given = len(scalars) + len(inputs)

        def body(*refs):
            kernel(*refs[: given - skip], *refs[given:-1])
            refs[-1][...] = jnp.zeros((8, 128), F32)

        result = pl.pallas_call(
            body,
            grid_spec=pltpu.PrefetchScalarGridSpec(
                num_scalar_prefetch=len(scalars),
                grid=grid,
                in_specs=in_specs,
                out_specs=[*out_specs, block(8, 128)],
            ),
            out_shape=[*outs, shape(8, 128)],
            cost_estimate=pl.CostEstimate(
                flops=int(share * flops), bytes_accessed=int(share * size), transcendentals=0
            ),
            compiler_params=pltpu.CompilerParams(vmem_limit_bytes=limit * 2**20),
        )(*scalars, *inputs)
        *result, self.token = result
        return result[0] if len(outs) == 1 else result


def copy_kernel(in_ref, out_ref):
    out_ref[...] = in_ref[...]


def columns(line, matrix, start, width):
    rows = matrix.shape[0]
    tile = width // 2
    return line.run(
        copy_kernel,
        (matrix,),
        (pl.BlockSpec((rows, tile), lambda n: (0, start // tile + n)),),
        (shape(rows, width, matrix.dtype),),
        (pl.BlockSpec((rows, tile), lambda n: (0, n)),),
        grid=(width // tile,),
    )


def turned(near_ref, far_ref, out_ref):
    rows = near_ref.shape[1]
    out_ref[:rows, :] = near_ref[...].T
    out_ref[rows:, :] = far_ref[...].T


def pack_two_kernel(place_ref, near_ref, far_ref, first_ref, rest_ref):
    step = pl.program_id(0)

    @pl.when(step == 0)
    def _():
        turned(near_ref, far_ref, first_ref)

    @pl.when(step > 0)
    def _():
        turned(near_ref, far_ref, rest_ref)


def pack_kernel(count, place_ref, near_ref, far_ref, *refs):
    turned(near_ref, far_ref, refs[count])
    for part_ref, copy_ref in zip(refs[:count], refs[count + 1 :]):
        copy_ref[...] = part_ref[...]


def pack(line, context, place, rows, cotangent=None, parts=()):
    tokens, width = context.shape

    def column(half, step, place):
        core, x, y = place[0], place[1], place[2]
        turn = jnp.where(core == 0, 2 * X - 1 - step, 1 + step)
        return (0, ((y + half) % HALVES) * (2 * X) + ((x + turn) % X) * 2 + core)

    def taken(start, size):
        tile = size // X
        return pl.BlockSpec((tokens, tile), lambda step, place: (0, start // tile + step))

    pair = 2 * rows
    if parts:
        kernel = functools.partial(pack_kernel, len(parts))
        outs = [shape(X * pair, tokens, BF16)]
        out_specs = [pl.BlockSpec((pair, tokens), lambda step, place: (step, 0))]
    else:
        kernel = pack_two_kernel
        outs = [shape(pair, tokens, BF16), shape((X - 1) * pair, tokens, BF16)]
        out_specs = [
            pl.BlockSpec((pair, tokens), lambda step, place: (0, 0)),
            pl.BlockSpec((pair, tokens), lambda step, place: (jnp.maximum(step - 1, 0), 0)),
        ]
    return line.run(
        kernel,
        (context, context, *[cotangent] * len(parts)),
        (
            pl.BlockSpec((tokens, rows), functools.partial(column, 0)),
            pl.BlockSpec((tokens, rows), functools.partial(column, 1)),
            *[taken(*part) for part in parts],
        ),
        [*outs, *[shape(tokens, size, BF16) for _, size in parts]],
        [*out_specs, *[taken(0, size) for _, size in parts]],
        grid=(X,),
        scalars=(place,),
    )


def both(own_lhs, other_lhs, own_rhs, other_rhs, part=slice(None)):
    total = jnp.dot(own_lhs[...], own_rhs[:, part], preferred_element_type=F32)
    return total + jnp.dot(other_lhs[...], other_rhs[:, part], preferred_element_type=F32)


def parts_of(ref):
    width = ref.shape[1]
    return [slice(start, start + 256) for start in range(0, width, 256)]


def first_kernel(own_lhs, other_lhs, own_rhs, other_rhs, code_ref):
    for part in parts_of(code_ref):
        code_ref[:, part] = encode(both(own_lhs, other_lhs, own_rhs, other_rhs, part))


def relay_kernel(own_lhs, other_lhs, own_rhs, other_rhs, arrived_ref, code_ref):
    for part in parts_of(code_ref):
        total = both(own_lhs, other_lhs, own_rhs, other_rhs, part) + decode(arrived_ref[:, part])
        code_ref[:, part] = encode(total)


def settle_kernel(own_lhs, other_lhs, own_rhs, other_rhs, arrived_ref, keep_ref, code_ref):
    rows = keep_ref.shape[0]
    for part in parts_of(code_ref):
        total = both(own_lhs, other_lhs, own_rhs, other_rhs, part) + decode(arrived_ref[:, part])
        keep_ref[:, part] = total[:rows]
        code_ref[:, part] = encode(total[rows:])


def crossed_kernel(own_lhs, other_lhs, own_rhs, other_rhs, rest_lhs, code_ref, out_ref):
    total = jnp.dot(own_lhs[...], own_rhs[...], preferred_element_type=F32)
    pair = other_lhs.shape[0]
    rows = pair // 2
    for s in range(X):
        lhs = other_lhs[...] if s == 0 else rest_lhs[(s - 1) * pair : s * pair, :]
        both_tokens = total[s * pair : (s + 1) * pair] + jnp.dot(
            lhs, other_rhs[...], preferred_element_type=F32
        )
        out_ref[s * rows : (s + 1) * rows, :] = both_tokens[:rows]
        code_ref[s * rows : (s + 1) * rows, :] = encode(both_tokens[rows:])


def product(line, kernel, lhs, own_cot, other_cot, start, step, rows, outs, arrived=None):
    tokens, width = other_cot.shape
    own_lhs, first_lhs, rest_lhs = lhs
    other_lhs, other_step = (rest_lhs, step - 1) if step else (first_lhs, 0)
    every = step is None
    inputs = [own_lhs, other_lhs, own_cot, other_cot]
    specs = [
        block(*own_lhs.shape) if every else block(rows, tokens, step),
        block(rows, tokens, other_step),
        pl.BlockSpec((tokens, TILE), lambda n: (0, start // TILE + n)),
        pl.BlockSpec((tokens, TILE), lambda n: (0, n)),
    ]
    if every:
        inputs.append(rest_lhs)
        specs.append(block(*rest_lhs.shape))
    if arrived is not None:
        inputs.append(arrived)
        specs.append(pl.BlockSpec((rows, TILE), lambda n: (0, n)))
    return line.run(
        kernel,
        inputs,
        specs,
        [shape(r, width, t) for r, t in outs],
        [pl.BlockSpec((r, TILE), lambda n: (0, n)) for r, _ in outs],
        grid=(width // TILE,),
        limit=28,
        flops=4 * (X * rows if every else rows) * tokens * width,
    )


def open_kernel(own_ref, crossed_ref, out_ref):
    out_ref[...] = encode(own_ref[...] + decode(crossed_ref[...]))


def pass_kernel(own_ref, crossed_ref, arrived_ref, out_ref):
    out_ref[...] = encode(own_ref[...] + decode(crossed_ref[...]) + decode(arrived_ref[...]))


def pass_on(line, own, crossed, step, arrived=None):
    width = own.shape[1]
    rows = own.shape[0] // X
    here = block(rows, width, step)
    arrived = [] if arrived is None else [arrived]
    return line.run(
        pass_kernel if arrived else open_kernel,
        (own, crossed, *arrived),
        (here, here, *[block(rows, width)] * len(arrived)),
        (shape(rows, width, BF16),),
        (block(rows, width),),
        limit=16,
    )


def three(value):
    high = value.astype(BF16).astype(F32)
    rest = value - high
    middle = rest.astype(BF16).astype(F32)
    low = rest - middle
    return jnp.concatenate([high, middle, low, jnp.zeros_like(low)], axis=0).astype(BF16)


def added(parts):
    rows = parts.shape[0] // 4
    return parts[:rows] + (parts[rows : 2 * rows] + parts[2 * rows : 3 * rows])


def edge_kernel(own_ref, next_ref, edge_ref, sums_ref, lowrank_ref):
    differ = own_ref[...].astype(F32) - next_ref[...].astype(F32)
    high = differ.astype(BF16)
    low = (differ - high.astype(F32)).astype(BF16)

    def times(rows, axes):
        parts = three(rows)
        return added(
            lax.dot_general(parts, high, axes, preferred_element_type=F32)
            + lax.dot_general(parts, low, axes, preferred_element_type=F32)
        )

    lowrank = times(edge_ref[...], LAST)
    lowrank_ref[...] = lowrank
    width = differ.shape[1]
    sums_ref[:, :width] = times(lowrank, (((1,), (0,)), ((), ())))
    rank, rows = lowrank.shape
    square = jnp.concatenate([lowrank, jnp.zeros((128 - rank, rows), F32)], axis=0)
    sums_ref[:, width:] = lax.dot_general(lowrank, square, LAST, precision=HIGH, preferred_element_type=F32)


def edge_sums(line, own, following, edge):
    rows, width = own.shape
    rank = edge.shape[0]
    return line.run(
        edge_kernel,
        (own, following, edge),
        (block(rows, width), block(rows, width), block(rank, width)),
        (shape(rank, width + 128), shape(rank, rows)),
        (block(rank, width + 128), block(rank, rows)),
    )


def plus_kernel(one_ref, two_ref, out_ref):
    out_ref[...] = one_ref[...] + two_ref[...]


def plus_ring_kernel(own_ref, one_ref, two_ref, three_ref, out_ref):
    out_ref[...] = (own_ref[...] + two_ref[...]) + (one_ref[...] + three_ref[...])


def combine(line, kernel, *arrays):
    return line.run(
        kernel,
        arrays,
        [block(*array.shape) for array in arrays],
        (shape(*arrays[0].shape),),
        (block(*arrays[0].shape),),
        limit=16,
    )


def solve_kernel(one_ref, two_ref, lowrank_ref, vectors_ref, packed_ref):
    rank = lowrank_ref.shape[0]
    width = vectors_ref.shape[1]
    gram = one_ref[:, width:] + two_ref[:, width:]
    right = one_ref[:, :width] + two_ref[:, :width]
    lowrank = lowrank_ref[...]
    row = lax.broadcasted_iota(jnp.int32, (rank, 1), 0)

    def step(matrix, k, factor, inverse):
        pivot = matrix[k : k + 1, :] * inverse
        return jnp.where(row == k, pivot, matrix - factor * pivot)

    for k in range(rank):
        inverse = 1.0 / jnp.sqrt(gram[k : k + 1, k : k + 1])
        factor = jnp.where(row > k, gram[:, k : k + 1] * inverse, 0.0)
        gram, right, lowrank = (step(m, k, factor, inverse) for m in (gram, right, lowrank))
    vectors_ref[...] = right
    packed_ref[:, :width] = right
    packed_ref[:, width:] = lowrank


def solve(line, one, two, lowrank):
    rank, rows = lowrank.shape
    width = one.shape[1] - 128
    return line.run(
        solve_kernel,
        (one, two, lowrank),
        (block(*one.shape), block(*one.shape), block(rank, rows)),
        (shape(rank, width), shape(rank, width + rows)),
        (block(rank, width), block(rank, width + rows)),
        limit=16,
    )


def mix_kernel(rate, weights_ref, right_ref, left_ref, right_basis, left_basis, keep_ref, code_ref, out_ref):
    def parts(value):
        high = value.astype(BF16)
        rest = value - high.astype(F32)
        middle = rest.astype(BF16)
        return high, middle, (rest - middle.astype(F32)).astype(BF16)

    b = parts(jnp.concatenate([right_basis[...], -left_basis[...]], axis=0))
    v = parts(jnp.concatenate([right_ref[...], left_ref[...]], axis=0))
    pairs = ((0, 0), (0, 1), (1, 0), (0, 2), (2, 0), (1, 1))
    approx = lax.dot_general(
        jnp.concatenate([b[i] for i, _ in pairs], axis=0),
        jnp.concatenate([v[j] for _, j in pairs], axis=0),
        (((0,), (0,)), ((), ())),
        preferred_element_type=F32,
    )
    mixed = weights_ref[...].astype(F32) - gossip_rate * approx
    width = keep_ref.shape[1]
    out_ref[:, :width] = mixed[:, :width] - rate * (keep_ref[...] + decode(code_ref[...]))
    out_ref[:, width:] = mixed[:, width:]


def mix(line, rate, weights, right, left, keep, code):
    rows, width = weights.shape
    rank = right.shape[0]
    vectors, whole = block(rank, width), block(rows, width)
    basis = block(rank, rows, 0, width // rows)
    return line.run(
        functools.partial(mix_kernel, rate),
        (weights, right, left, right, left, keep, code),
        (whole, vectors, vectors, basis, basis, block(*keep.shape), block(*code.shape)),
        (shape(rows, width),),
        (whole,),
        limit=20,
    )


def finish_kernel(rate, start, counts, mixed_ref, *refs):
    out_ref = refs[-1]
    out_ref[:, :start] = mixed_ref[:, :start]
    used = 0
    for count in counts:
        total = refs[used][...]
        for code in refs[used + 1 : used + count]:
            total += decode(code[...])
        part = slice(start, start + total.shape[1])
        out_ref[:, part] = mixed_ref[:, part] - rate * total
        start, used = part.stop, used + count


def finish(line, rate, start, mixed, parts):
    rows = mixed.shape[0]
    flat = [array for group in parts for array in group]
    whole = block(*mixed.shape)
    return line.run(
        functools.partial(finish_kernel, rate, start, [len(group) for group in parts]),
        (mixed, *flat),
        (whole, *[block(rows, array.shape[1], array.shape[0] // rows - 1) for array in flat]),
        (shape(*mixed.shape),),
        (whole,),
        limit=20,
    )


def local(context, cotangent, weights, edge_vectors):
    groups = lax.axis_size("fsdp")
    replicas = lax.axis_size("blk")
    context, cotangent, weights, edge = context[0], cotangent[0], weights[0], edge_vectors[0]
    tokens, width = cotangent.shape
    rows = weights.shape[0]
    pair = HALVES * rows
    b_width, a_width = WIDTHS
    a_start, c_start = b_width, b_width + a_width
    c_width = width - c_start

    place = lax.axis_index("fsdp")
    core, x, y = place % 2, (place // 2) % X, place // (2 * X)
    own_place = jnp.stack([core, x, y]).astype(jnp.int32)
    other_place = jnp.stack([1 - core, x, y]).astype(jnp.int32)

    def move(value, target):
        return lax.ppermute(value, "fsdp", [(i, target(i)) for i in range(groups)])

    def flip(bit):
        return lambda i: i ^ bit

    other_core, other_half = flip(1), flip(2 * X)

    def along(by):
        def target(i):
            ahead = by if i % 2 == 0 else X - by
            return i // (2 * X) * (2 * X) + ((i // 2 + ahead) % X) * 2 + i % 2

        return target

    def turn(value, by):
        return lax.ppermute(value, "blk", [(i, (i + by) % replicas) for i in range(replicas)])

    line = Line()

    line.name = "pack1"
    first_lhs, rest_lhs = pack(line, context, other_place, rows)
    line.name = "slice"
    b_other = move(columns(line, cotangent, 0, b_width), other_core)
    first_lhs, rest_lhs = move(first_lhs, other_core), move(rest_lhs, other_core)
    line.name = "pack2"
    parts = [(a_start, a_width), (c_start, c_width)]
    own_lhs, a_cot, c_cot = pack(line, context, own_place, rows, cotangent, parts)
    a_other, c_other = move(a_cot, other_core), move(c_cot, other_core)
    times = functools.partial(product, line, lhs=(own_lhs, first_lhs, rest_lhs), own_cot=cotangent)
    b_part = dict(other_cot=b_other, start=0, rows=pair)
    a_part = dict(other_cot=a_other, start=a_start, rows=pair)
    whole = [(pair, BF16)]
    halves = [(rows, F32), (rows, BF16)]

    line.name = "b0"
    following = turn(weights, -1)
    b1 = move(times(first_kernel, **b_part, step=0, outs=whole), along(1))
    rate = learn_rate / math.sqrt(groups * tokens)
    have = {"b1": b1}

    def step_a0():
        have["a1"] = move(times(first_kernel, **a_part, step=0, outs=whole), along(1))

    def step_c():
        outs = [(X * rows, BF16), (X * rows, F32)]
        part = dict(other_cot=c_other, start=c_start, step=None, rows=pair)
        code, have["c_own"] = times(crossed_kernel, **part, outs=outs)
        have["c_cross"] = move(code, other_half)

    def step_edge():
        have["sums"], have["lowrank"] = edge_sums(line, weights, following, edge)
        have["sums_core"] = move(have["sums"], other_core)

    def step_add():
        have["sums"] = combine(line, plus_kernel, have["sums"], have["sums_core"])
        have["sums_x"] = [move(have["sums"], flip(2 * by)) for by in (1, 2, 3)]

    def step_sum_x():
        have["sums"] = combine(line, plus_ring_kernel, have["sums"], *have["sums_x"])
        have["sums_y"] = move(have["sums"], other_half)

    def step_solve():
        have["vectors"], have["right"] = solve(line, have["sums"], have["sums_y"], have["lowrank"])
        have["left"] = turn(have["right"], 1)

    def step_mix():
        have["mixed"] = mix(line, rate, weights, have["right"], have["left"], *have["b_last"])

    def step_ring(name, part, step):
        before, after = f"{name}{step}", f"{name}{step + 1}"
        code = times(relay_kernel, **part, step=step, outs=whole, arrived=have[before])
        have[after] = move(code, along(1))

    def step_settle(name, part):
        keep, send = times(settle_kernel, **part, step=X - 1, outs=halves, arrived=have[f"{name}{X - 1}"])
        have[f"{name}_last"] = keep, move(send, other_half)

    def step_pass(step):
        code = pass_on(line, have["c_own"], have["c_cross"], step, have.get(f"c{step}"))
        have[f"c{step + 1}"] = move(code, along(1))

    steps = dict(
        a0=step_a0,
        c=step_c,
        edge=step_edge,
        add=step_add,
        sum_x=step_sum_x,
        solve=step_solve,
        mix=step_mix,
        b1=lambda: step_ring("b", b_part, 1),
        b2=lambda: step_ring("b", b_part, 2),
        b3=lambda: step_settle("b", b_part),
        a1=lambda: step_ring("a", a_part, 1),
        a2=lambda: step_ring("a", a_part, 2),
        a3=lambda: step_settle("a", a_part),
        c0=lambda: step_pass(0),
        c1=lambda: step_pass(1),
        c2=lambda: step_pass(2),
    )
    for name in ORDER:
        line.name = name
        steps[name]()
    line.name = "finish"
    last = have["c_own"], have["c_cross"], have["c3"]
    new_weights, new_vectors = finish(line, rate, a_start, have["mixed"], [have["a_last"], last]), have["vectors"]
    return (new_weights[None], new_vectors[None])


def solution(mesh):
    return jax.shard_map(
        local,
        mesh=mesh,
        in_specs=(
            P("blk", "fsdp", None),
            P("blk", "fsdp", None),
            P("blk", "fsdp", None),
            P("blk", None, None),
        ),
        out_specs=(P("blk", "fsdp", None), P("blk", None, None)),
        check_vma=False,
    )
```

```python
import functools
import math

import jax
import jax.numpy as jnp
from jax import lax
from jax.experimental import pallas as pl
from jax.experimental.pallas import tpu as pltpu
from jax.sharding import PartitionSpec as P

learn_rate = 0.5
gossip_rate = 0.5

X = 4
HALVES = 2
TILE = 512
POWER = 9
TINY = 1e-37
CODE_SCALE = 2.0**-5

ORDER = ("a0", "c", "b1", "a1", "edge", "b2", "add", "a2", "sum_x", "b3", "solve", "spread", "mix", "a3")
HIGH = lax.Precision.HIGHEST
SHARES = dict(pack1=1.0, slice=1.0, pack2=1.0, b0=30.0, a0=1.0, c=3.0, b1=3.0, b2=3.0)
WIDTHS = (1536, 1536)
F32 = jnp.float32
BF16 = jnp.bfloat16
LAST = (((1,), (1,)), ((), ()))


def encode(total):
    z = total * CODE_SCALE
    z2 = z * z
    z4 = z2 * z2
    return (z4 * z4 * z).astype(BF16)


def decode(code):
    code = code.astype(F32)
    size = jnp.log(jnp.maximum(jnp.abs(code), TINY))
    return code * lax.exp2(size * ((1.0 / POWER - 1.0) / math.log(2.0)) - math.log2(CODE_SCALE))


def shape(rows, width, dtype=F32):
    return jax.ShapeDtypeStruct((rows, width), dtype)


def block(rows, width, row=0, column=0):
    return pl.BlockSpec((rows, width), lambda *_: (row, column))


class Line:
    def __init__(self):
        self.token = None
        self.name = None

    def run(self, kernel, inputs, in_specs, outs, out_specs, grid=(1,), scalars=(), limit=24, flops=0):
        share = SHARES.get(self.name, 10.0)
        inputs, in_specs = list(inputs), list(in_specs)
        size = sum(math.prod(a.shape) * jnp.dtype(a.dtype).itemsize for a in (*inputs, *outs))
        waits = [] if self.token is None else [self.token]
        skip = len(waits)
        inputs += waits
        in_specs += [pl.BlockSpec(memory_space=pl.ANY)] * skip
        given = len(scalars) + len(inputs)

        def body(*refs):
            kernel(*refs[: given - skip], *refs[given:-1])
            refs[-1][...] = jnp.zeros((8, 128), F32)

        result = pl.pallas_call(
            body,
            grid_spec=pltpu.PrefetchScalarGridSpec(
                num_scalar_prefetch=len(scalars),
                grid=grid,
                in_specs=in_specs,
                out_specs=[*out_specs, block(8, 128)],
            ),
            out_shape=[*outs, shape(8, 128)],
            cost_estimate=pl.CostEstimate(
                flops=int(share * flops), bytes_accessed=int(share * size), transcendentals=0
            ),
            compiler_params=pltpu.CompilerParams(vmem_limit_bytes=limit * 2**20),
        )(*scalars, *inputs)
        *result, self.token = result
        return result[0] if len(outs) == 1 else result


def copy_kernel(in_ref, out_ref):
    out_ref[...] = in_ref[...]


def columns(line, matrix, start, width):
    rows = matrix.shape[0]
    tile = width // 2
    return line.run(
        copy_kernel,
        (matrix,),
        (pl.BlockSpec((rows, tile), lambda n: (0, start // tile + n)),),
        (shape(rows, width, matrix.dtype),),
        (pl.BlockSpec((rows, tile), lambda n: (0, n)),),
        grid=(width // tile,),
    )


def turned(near_ref, far_ref, out_ref):
    rows = near_ref.shape[1]
    out_ref[:rows, :] = near_ref[...].T
    out_ref[rows:, :] = far_ref[...].T


def pack_two_kernel(place_ref, near_ref, far_ref, first_ref, rest_ref):
    step = pl.program_id(0)

    @pl.when(step == 0)
    def _():
        turned(near_ref, far_ref, first_ref)

    @pl.when(step > 0)
    def _():
        turned(near_ref, far_ref, rest_ref)


def pack_kernel(count, place_ref, near_ref, far_ref, *refs):
    turned(near_ref, far_ref, refs[count])
    for part_ref, copy_ref in zip(refs[:count], refs[count + 1 :]):
        copy_ref[...] = part_ref[...]


def pack(line, context, place, rows, cotangent=None, parts=()):
    tokens, width = context.shape

    def column(half, step, place):
        core, x, y = place[0], place[1], place[2]
        turn = jnp.where(core == 0, 2 * X - 1 - step, 1 + step)
        return (0, ((y + half) % HALVES) * (2 * X) + ((x + turn) % X) * 2 + core)

    def taken(start, size):
        tile = size // X
        return pl.BlockSpec((tokens, tile), lambda step, place: (0, start // tile + step))

    pair = 2 * rows
    if parts:
        kernel = functools.partial(pack_kernel, len(parts))
        outs = [shape(X * pair, tokens, BF16)]
        out_specs = [pl.BlockSpec((pair, tokens), lambda step, place: (step, 0))]
    else:
        kernel = pack_two_kernel
        outs = [shape(pair, tokens, BF16), shape((X - 1) * pair, tokens, BF16)]
        out_specs = [
            pl.BlockSpec((pair, tokens), lambda step, place: (0, 0)),
            pl.BlockSpec((pair, tokens), lambda step, place: (jnp.maximum(step - 1, 0), 0)),
        ]
    return line.run(
        kernel,
        (context, context, *[cotangent] * len(parts)),
        (
            pl.BlockSpec((tokens, rows), functools.partial(column, 0)),
            pl.BlockSpec((tokens, rows), functools.partial(column, 1)),
            *[taken(*part) for part in parts],
        ),
        [*outs, *[shape(tokens, size, BF16) for _, size in parts]],
        [*out_specs, *[taken(0, size) for _, size in parts]],
        grid=(X,),
        scalars=(place,),
    )


def both(own_lhs, other_lhs, own_rhs, other_rhs, part=slice(None)):
    total = jnp.dot(own_lhs[...], own_rhs[:, part], preferred_element_type=F32)
    return total + jnp.dot(other_lhs[...], other_rhs[:, part], preferred_element_type=F32)


def parts_of(ref):
    width = ref.shape[1]
    return [slice(start, start + 256) for start in range(0, width, 256)]


def first_kernel(own_lhs, other_lhs, own_rhs, other_rhs, code_ref):
    for part in parts_of(code_ref):
        code_ref[:, part] = encode(both(own_lhs, other_lhs, own_rhs, other_rhs, part))


def relay_kernel(own_lhs, other_lhs, own_rhs, other_rhs, arrived_ref, code_ref):
    for part in parts_of(code_ref):
        total = both(own_lhs, other_lhs, own_rhs, other_rhs, part) + decode(arrived_ref[:, part])
        code_ref[:, part] = encode(total)


def settle_kernel(own_lhs, other_lhs, own_rhs, other_rhs, arrived_ref, keep_ref, code_ref):
    rows = keep_ref.shape[0]
    for part in parts_of(code_ref):
        total = both(own_lhs, other_lhs, own_rhs, other_rhs, part) + decode(arrived_ref[:, part])
        keep_ref[:, part] = total[:rows]
        code_ref[:, part] = encode(total[rows:])


def crossed_kernel(own_lhs, other_lhs, own_rhs, other_rhs, rest_lhs, code_ref, out_ref):
    total = jnp.dot(own_lhs[...], own_rhs[...], preferred_element_type=F32)
    pair = other_lhs.shape[0]
    rows = pair // 2
    for s in range(X):
        lhs = other_lhs[...] if s == 0 else rest_lhs[(s - 1) * pair : s * pair, :]
        both_tokens = total[s * pair : (s + 1) * pair] + jnp.dot(
            lhs, other_rhs[...], preferred_element_type=F32
        )
        out_ref[s * rows : (s + 1) * rows, :] = both_tokens[:rows]
        code_ref[s * rows : (s + 1) * rows, :] = encode(both_tokens[rows:])


def product(line, kernel, lhs, own_cot, other_cot, start, step, rows, outs, arrived=None):
    tokens, width = other_cot.shape
    own_lhs, first_lhs, rest_lhs = lhs
    other_lhs, other_step = (rest_lhs, step - 1) if step else (first_lhs, 0)
    every = step is None
    inputs = [own_lhs, other_lhs, own_cot, other_cot]
    specs = [
        block(*own_lhs.shape) if every else block(rows, tokens, step),
        block(rows, tokens, other_step),
        pl.BlockSpec((tokens, TILE), lambda n: (0, start // TILE + n)),
        pl.BlockSpec((tokens, TILE), lambda n: (0, n)),
    ]
    if every:
        inputs.append(rest_lhs)
        specs.append(block(*rest_lhs.shape))
    if arrived is not None:
        inputs.append(arrived)
        specs.append(pl.BlockSpec((rows, TILE), lambda n: (0, n)))
    return line.run(
        kernel,
        inputs,
        specs,
        [shape(r, width, t) for r, t in outs],
        [pl.BlockSpec((r, TILE), lambda n: (0, n)) for r, _ in outs],
        grid=(width // TILE,),
        limit=28,
        flops=4 * (X * rows if every else rows) * tokens * width,
    )


def spread_kernel(own_ref, crossed_ref, *out_refs):
    rows = out_refs[0].shape[0]
    for s, out_ref in enumerate(out_refs):
        part = slice(s * rows, (s + 1) * rows)
        total = own_ref[part, :] + decode(crossed_ref[part, :])
        out_ref[...] = encode(total) if s < X - 1 else total


def spread(line, own, crossed):
    width = own.shape[1]
    rows = own.shape[0] // X
    whole = block(X * rows, width)
    return line.run(
        spread_kernel,
        (own, crossed),
        (whole, whole),
        [shape(rows, width, BF16)] * (X - 1) + [shape(rows, width)],
        [block(rows, width)] * X,
        limit=16,
    )


def three(value):
    high = value.astype(BF16).astype(F32)
    rest = value - high
    middle = rest.astype(BF16).astype(F32)
    low = rest - middle
    return jnp.concatenate([high, middle, low, jnp.zeros_like(low)], axis=0).astype(BF16)


def added(parts):
    rows = parts.shape[0] // 4
    return parts[:rows] + (parts[rows : 2 * rows] + parts[2 * rows : 3 * rows])


def edge_kernel(own_ref, next_ref, edge_ref, sums_ref, lowrank_ref):
    differ = own_ref[...].astype(F32) - next_ref[...].astype(F32)
    high = differ.astype(BF16)
    low = (differ - high.astype(F32)).astype(BF16)

    def times(rows, axes):
        parts = three(rows)
        return added(
            lax.dot_general(parts, high, axes, preferred_element_type=F32)
            + lax.dot_general(parts, low, axes, preferred_element_type=F32)
        )

    lowrank = times(edge_ref[...], LAST)
    lowrank_ref[...] = lowrank
    width = differ.shape[1]
    sums_ref[:, :width] = times(lowrank, (((1,), (0,)), ((), ())))
    rank, rows = lowrank.shape
    square = jnp.concatenate([lowrank, jnp.zeros((128 - rank, rows), F32)], axis=0)
    sums_ref[:, width:] = lax.dot_general(lowrank, square, LAST, precision=HIGH, preferred_element_type=F32)


def edge_sums(line, own, following, edge):
    rows, width = own.shape
    rank = edge.shape[0]
    return line.run(
        edge_kernel,
        (own, following, edge),
        (block(rows, width), block(rows, width), block(rank, width)),
        (shape(rank, width + 128), shape(rank, rows)),
        (block(rank, width + 128), block(rank, rows)),
    )


def plus_kernel(one_ref, two_ref, out_ref):
    out_ref[...] = one_ref[...] + two_ref[...]


def plus_ring_kernel(own_ref, one_ref, two_ref, three_ref, out_ref):
    out_ref[...] = (own_ref[...] + two_ref[...]) + (one_ref[...] + three_ref[...])


def combine(line, kernel, *arrays):
    return line.run(
        kernel,
        arrays,
        [block(*array.shape) for array in arrays],
        (shape(*arrays[0].shape),),
        (block(*arrays[0].shape),),
        limit=16,
    )


def solve_kernel(one_ref, two_ref, lowrank_ref, vectors_ref, packed_ref):
    rank = lowrank_ref.shape[0]
    width = vectors_ref.shape[1]
    gram = one_ref[:, width:] + two_ref[:, width:]
    right = one_ref[:, :width] + two_ref[:, :width]
    lowrank = lowrank_ref[...]
    row = lax.broadcasted_iota(jnp.int32, (rank, 1), 0)

    def step(matrix, k, factor, inverse):
        pivot = matrix[k : k + 1, :] * inverse
        return jnp.where(row == k, pivot, matrix - factor * pivot)

    for k in range(rank):
        inverse = 1.0 / jnp.sqrt(gram[k : k + 1, k : k + 1])
        factor = jnp.where(row > k, gram[:, k : k + 1] * inverse, 0.0)
        gram, right, lowrank = (step(m, k, factor, inverse) for m in (gram, right, lowrank))
    vectors_ref[...] = right
    packed_ref[:, :width] = right
    packed_ref[:, width:] = lowrank


def solve(line, one, two, lowrank):
    rank, rows = lowrank.shape
    width = one.shape[1] - 128
    return line.run(
        solve_kernel,
        (one, two, lowrank),
        (block(*one.shape), block(*one.shape), block(rank, rows)),
        (shape(rank, width), shape(rank, width + rows)),
        (block(rank, width), block(rank, width + rows)),
        limit=16,
    )


def mix_kernel(weights_ref, right_ref, left_ref, right_basis, left_basis, out_ref):
    def parts(value):
        high = value.astype(BF16)
        rest = value - high.astype(F32)
        middle = rest.astype(BF16)
        return high, middle, (rest - middle.astype(F32)).astype(BF16)

    b = parts(jnp.concatenate([right_basis[...], -left_basis[...]], axis=0))
    v = parts(jnp.concatenate([right_ref[...], left_ref[...]], axis=0))
    pairs = ((0, 0), (0, 1), (1, 0), (0, 2), (2, 0), (1, 1))
    approx = lax.dot_general(
        jnp.concatenate([b[i] for i, _ in pairs], axis=0),
        jnp.concatenate([v[j] for _, j in pairs], axis=0),
        (((0,), (0,)), ((), ())),
        preferred_element_type=F32,
    )
    out_ref[...] = weights_ref[...].astype(F32) - gossip_rate * approx


def mix(line, weights, right, left):
    rows, width = weights.shape
    rank = right.shape[0]
    vectors, whole = block(rank, width), block(rows, width)
    basis = block(rank, rows, 0, width // rows)
    return line.run(
        mix_kernel,
        (weights, right, left, right, left),
        (whole, vectors, vectors, basis, basis),
        (shape(rows, width),),
        (whole,),
        limit=20,
    )


def finish_kernel(rate, counts, mixed_ref, *refs):
    out_ref = refs[-1]
    start = used = 0
    for count in counts:
        total = refs[used][...]
        for code in refs[used + 1 : used + count]:
            total += decode(code[...])
        part = slice(start, start + total.shape[1])
        out_ref[:, part] = mixed_ref[:, part] - rate * total
        start, used = part.stop, used + count


def finish(line, rate, mixed, parts):
    rows = mixed.shape[0]
    flat = [array for group in parts for array in group]
    whole = block(*mixed.shape)
    return line.run(
        functools.partial(finish_kernel, rate, [len(group) for group in parts]),
        (mixed, *flat),
        (whole, *[block(rows, array.shape[1], array.shape[0] // rows - 1) for array in flat]),
        (shape(*mixed.shape),),
        (whole,),
        limit=20,
    )


def local(context, cotangent, weights, edge_vectors):
    groups = lax.axis_size("fsdp")
    replicas = lax.axis_size("blk")
    context, cotangent, weights, edge = context[0], cotangent[0], weights[0], edge_vectors[0]
    tokens, width = cotangent.shape
    rows = weights.shape[0]
    pair = HALVES * rows
    b_width, a_width = WIDTHS
    a_start, c_start = b_width, b_width + a_width
    c_width = width - c_start

    place = lax.axis_index("fsdp")
    core, x, y = place % 2, (place // 2) % X, place // (2 * X)
    own_place = jnp.stack([core, x, y]).astype(jnp.int32)
    other_place = jnp.stack([1 - core, x, y]).astype(jnp.int32)

    def move(value, target):
        return lax.ppermute(value, "fsdp", [(i, target(i)) for i in range(groups)])

    def flip(bit):
        return lambda i: i ^ bit

    other_core, other_half = flip(1), flip(2 * X)

    def along(by):
        def target(i):
            ahead = by if i % 2 == 0 else X - by
            return i // (2 * X) * (2 * X) + ((i // 2 + ahead) % X) * 2 + i % 2

        return target

    def turn(value, by):
        return lax.ppermute(value, "blk", [(i, (i + by) % replicas) for i in range(replicas)])

    line = Line()

    line.name = "pack1"
    first_lhs, rest_lhs = pack(line, context, other_place, rows)
    line.name = "slice"
    b_other = move(columns(line, cotangent, 0, b_width), other_core)
    first_lhs, rest_lhs = move(first_lhs, other_core), move(rest_lhs, other_core)
    line.name = "pack2"
    parts = [(a_start, a_width), (c_start, c_width)]
    own_lhs, a_cot, c_cot = pack(line, context, own_place, rows, cotangent, parts)
    a_other, c_other = move(a_cot, other_core), move(c_cot, other_core)
    times = functools.partial(product, line, lhs=(own_lhs, first_lhs, rest_lhs), own_cot=cotangent)
    b_part = dict(other_cot=b_other, start=0, rows=pair)
    a_part = dict(other_cot=a_other, start=a_start, rows=pair)
    whole = [(pair, BF16)]
    halves = [(rows, F32), (rows, BF16)]

    line.name = "b0"
    following = turn(weights, -1)
    b1 = move(times(first_kernel, **b_part, step=0, outs=whole), along(1))
    rate = learn_rate / math.sqrt(groups * tokens)
    have = {"b1": b1}

    def step_a0():
        have["a1"] = move(times(first_kernel, **a_part, step=0, outs=whole), along(1))

    def step_c():
        outs = [(X * rows, BF16), (X * rows, F32)]
        part = dict(other_cot=c_other, start=c_start, step=None, rows=pair)
        code, have["c_own"] = times(crossed_kernel, **part, outs=outs)
        have["c_cross"] = move(code, other_half)

    def step_edge():
        have["sums"], have["lowrank"] = edge_sums(line, weights, following, edge)
        have["sums_core"] = move(have["sums"], other_core)

    def step_add():
        have["sums"] = combine(line, plus_kernel, have["sums"], have["sums_core"])
        have["sums_x"] = [move(have["sums"], flip(2 * by)) for by in (1, 2, 3)]

    def step_sum_x():
        have["sums"] = combine(line, plus_ring_kernel, have["sums"], *have["sums_x"])
        have["sums_y"] = move(have["sums"], other_half)

    def step_solve():
        have["vectors"], have["right"] = solve(line, have["sums"], have["sums_y"], have["lowrank"])
        have["left"] = turn(have["right"], 1)

    def step_mix():
        have["mixed"] = mix(line, weights, have["right"], have["left"])

    def step_ring(name, part, step):
        before, after = f"{name}{step}", f"{name}{step + 1}"
        code = times(relay_kernel, **part, step=step, outs=whole, arrived=have[before])
        have[after] = move(code, along(1))

    def step_settle(name, part):
        keep, send = times(settle_kernel, **part, step=X - 1, outs=halves, arrived=have[f"{name}{X - 1}"])
        have[f"{name}_last"] = keep, move(send, other_half)

    def step_spread():
        *codes, keep = spread(line, have["c_own"], have["c_cross"])
        have["c_last"] = keep, *[move(code, along(X - 1 - s)) for s, code in enumerate(codes)]

    steps = dict(
        a0=step_a0,
        c=step_c,
        edge=step_edge,
        add=step_add,
        sum_x=step_sum_x,
        solve=step_solve,
        mix=step_mix,
        b1=lambda: step_ring("b", b_part, 1),
        b2=lambda: step_ring("b", b_part, 2),
        b3=lambda: step_settle("b", b_part),
        a1=lambda: step_ring("a", a_part, 1),
        a2=lambda: step_ring("a", a_part, 2),
        a3=lambda: step_settle("a", a_part),
        spread=step_spread,
    )
    for name in ORDER:
        line.name = name
        steps[name]()
    line.name = "finish"
    new_weights = finish(line, rate, have["mixed"], [have["b_last"], have["a_last"], have["c_last"]])
    new_vectors = have["vectors"]
    return (new_weights[None], new_vectors[None])


def solution(mesh):
    return jax.shard_map(
        local,
        mesh=mesh,
        in_specs=(
            P("blk", "fsdp", None),
            P("blk", "fsdp", None),
            P("blk", "fsdp", None),
            P("blk", None, None),
        ),
        out_specs=(P("blk", "fsdp", None), P("blk", None, None)),
        check_vma=False,
    )
```

```python
import functools
import math

import jax
import jax.numpy as jnp
from jax import lax
from jax.experimental import pallas as pl
from jax.experimental.pallas import tpu as pltpu
from jax.sharding import PartitionSpec as P

learn_rate = 0.5
gossip_rate = 0.5

X = 4
HALVES = 2
TILE = 512
POWER = 9
TINY = 1e-37
CODE_SCALE = 2.0**-5

ORDER = ("a0", "c", "b1", "a1", "edge", "b2", "add", "a2", "sum_x", "b3", "solve", "spread", "mix", "a3")
HIGH = lax.Precision.HIGHEST
SHARES = dict(pack1=1.0, slice=1.0, pack2=1.0, b0=30.0, a0=1.0, c=3.0, b1=3.0, b2=3.0)
WIDTHS = (1536, 1536)
F32 = jnp.float32
BF16 = jnp.bfloat16
LAST = (((1,), (1,)), ((), ()))


def encode(total):
    z = total * CODE_SCALE
    z2 = z * z
    z4 = z2 * z2
    return (z4 * z4 * z).astype(BF16)


def decode(code):
    code = code.astype(F32)
    size = jnp.log(jnp.maximum(jnp.abs(code), TINY))
    return code * lax.exp2(size * ((1.0 / POWER - 1.0) / math.log(2.0)) - math.log2(CODE_SCALE))


def shape(rows, width, dtype=F32):
    return jax.ShapeDtypeStruct((rows, width), dtype)


def block(rows, width, row=0, column=0):
    return pl.BlockSpec((rows, width), lambda *_: (row, column))


class Line:
    def __init__(self):
        self.token = None
        self.name = None
        self.extra = []

    def after(self, *arrays):
        self.extra += arrays

    def run(self, kernel, inputs, in_specs, outs, out_specs, grid=(1,), scalars=(), limit=24, flops=0):
        share = SHARES.get(self.name, 10.0)
        inputs, in_specs = list(inputs), list(in_specs)
        size = sum(math.prod(a.shape) * jnp.dtype(a.dtype).itemsize for a in (*inputs, *outs))
        waits = [*self.extra, *([] if self.token is None else [self.token])]
        self.extra, skip = [], len(waits)
        inputs += waits
        in_specs += [pl.BlockSpec(memory_space=pl.ANY)] * skip
        given = len(scalars) + len(inputs)

        def body(*refs):
            kernel(*refs[: given - skip], *refs[given:-1])
            refs[-1][...] = jnp.zeros((8, 128), F32)

        result = pl.pallas_call(
            body,
            grid_spec=pltpu.PrefetchScalarGridSpec(
                num_scalar_prefetch=len(scalars),
                grid=grid,
                in_specs=in_specs,
                out_specs=[*out_specs, block(8, 128)],
            ),
            out_shape=[*outs, shape(8, 128)],
            cost_estimate=pl.CostEstimate(
                flops=int(share * flops), bytes_accessed=int(share * size), transcendentals=0
            ),
            compiler_params=pltpu.CompilerParams(vmem_limit_bytes=limit * 2**20),
        )(*scalars, *inputs)
        *result, self.token = result
        return result[0] if len(outs) == 1 else result


def copy_kernel(in_ref, out_ref):
    out_ref[...] = in_ref[...]


def columns(line, matrix, start, width):
    rows = matrix.shape[0]
    tile = width // 2
    return line.run(
        copy_kernel,
        (matrix,),
        (pl.BlockSpec((rows, tile), lambda n: (0, start // tile + n)),),
        (shape(rows, width, matrix.dtype),),
        (pl.BlockSpec((rows, tile), lambda n: (0, n)),),
        grid=(width // tile,),
    )


def turned(near_ref, far_ref, out_ref):
    rows = near_ref.shape[1]
    out_ref[:rows, :] = near_ref[...].T
    out_ref[rows:, :] = far_ref[...].T


def pack_two_kernel(place_ref, near_ref, far_ref, first_ref, rest_ref):
    step = pl.program_id(0)

    @pl.when(step == 0)
    def _():
        turned(near_ref, far_ref, first_ref)

    @pl.when(step > 0)
    def _():
        turned(near_ref, far_ref, rest_ref)


def pack_kernel(count, place_ref, near_ref, far_ref, *refs):
    turned(near_ref, far_ref, refs[count])
    for part_ref, copy_ref in zip(refs[:count], refs[count + 1 :]):
        copy_ref[...] = part_ref[...]


def pack(line, context, place, rows, cotangent=None, parts=()):
    tokens, width = context.shape

    def column(half, step, place):
        core, x, y = place[0], place[1], place[2]
        turn = jnp.where(core == 0, 2 * X - 1 - step, 1 + step)
        return (0, ((y + half) % HALVES) * (2 * X) + ((x + turn) % X) * 2 + core)

    def taken(start, size):
        tile = size // X
        return pl.BlockSpec((tokens, tile), lambda step, place: (0, start // tile + step))

    pair = 2 * rows
    if parts:
        kernel = functools.partial(pack_kernel, len(parts))
        outs = [shape(X * pair, tokens, BF16)]
        out_specs = [pl.BlockSpec((pair, tokens), lambda step, place: (step, 0))]
    else:
        kernel = pack_two_kernel
        outs = [shape(pair, tokens, BF16), shape((X - 1) * pair, tokens, BF16)]
        out_specs = [
            pl.BlockSpec((pair, tokens), lambda step, place: (0, 0)),
            pl.BlockSpec((pair, tokens), lambda step, place: (jnp.maximum(step - 1, 0), 0)),
        ]
    return line.run(
        kernel,
        (context, context, *[cotangent] * len(parts)),
        (
            pl.BlockSpec((tokens, rows), functools.partial(column, 0)),
            pl.BlockSpec((tokens, rows), functools.partial(column, 1)),
            *[taken(*part) for part in parts],
        ),
        [*outs, *[shape(tokens, size, BF16) for _, size in parts]],
        [*out_specs, *[taken(0, size) for _, size in parts]],
        grid=(X,),
        scalars=(place,),
    )


def both(own_lhs, other_lhs, own_rhs, other_rhs, part=slice(None)):
    total = jnp.dot(own_lhs[...], own_rhs[:, part], preferred_element_type=F32)
    return total + jnp.dot(other_lhs[...], other_rhs[:, part], preferred_element_type=F32)


def parts_of(ref):
    width = ref.shape[1]
    return [slice(start, start + 256) for start in range(0, width, 256)]


def first_kernel(own_lhs, other_lhs, own_rhs, other_rhs, code_ref):
    for part in parts_of(code_ref):
        code_ref[:, part] = encode(both(own_lhs, other_lhs, own_rhs, other_rhs, part))


def relay_kernel(own_lhs, other_lhs, own_rhs, other_rhs, arrived_ref, code_ref):
    for part in parts_of(code_ref):
        total = both(own_lhs, other_lhs, own_rhs, other_rhs, part) + decode(arrived_ref[:, part])
        code_ref[:, part] = encode(total)


def settle_kernel(own_lhs, other_lhs, own_rhs, other_rhs, arrived_ref, keep_ref, code_ref):
    rows = keep_ref.shape[0]
    for part in parts_of(code_ref):
        total = both(own_lhs, other_lhs, own_rhs, other_rhs, part) + decode(arrived_ref[:, part])
        keep_ref[:, part] = total[:rows]
        code_ref[:, part] = encode(total[rows:])


def crossed_kernel(own_lhs, other_lhs, own_rhs, other_rhs, rest_lhs, code_ref, out_ref):
    total = jnp.dot(own_lhs[...], own_rhs[...], preferred_element_type=F32)
    pair = other_lhs.shape[0]
    rows = pair // 2
    for s in range(X):
        lhs = other_lhs[...] if s == 0 else rest_lhs[(s - 1) * pair : s * pair, :]
        both_tokens = total[s * pair : (s + 1) * pair] + jnp.dot(
            lhs, other_rhs[...], preferred_element_type=F32
        )
        out_ref[s * rows : (s + 1) * rows, :] = both_tokens[:rows]
        code_ref[s * rows : (s + 1) * rows, :] = encode(both_tokens[rows:])


def product(line, kernel, lhs, own_cot, other_cot, start, step, rows, outs, arrived=None):
    tokens, width = other_cot.shape
    own_lhs, first_lhs, rest_lhs = lhs
    other_lhs, other_step = (rest_lhs, step - 1) if step else (first_lhs, 0)
    every = step is None
    inputs = [own_lhs, other_lhs, own_cot, other_cot]
    specs = [
        block(*own_lhs.shape) if every else block(rows, tokens, step),
        block(rows, tokens, other_step),
        pl.BlockSpec((tokens, TILE), lambda n: (0, start // TILE + n)),
        pl.BlockSpec((tokens, TILE), lambda n: (0, n)),
    ]
    if every:
        inputs.append(rest_lhs)
        specs.append(block(*rest_lhs.shape))
    if arrived is not None:
        inputs.append(arrived)
        specs.append(pl.BlockSpec((rows, TILE), lambda n: (0, n)))
    return line.run(
        kernel,
        inputs,
        specs,
        [shape(r, width, t) for r, t in outs],
        [pl.BlockSpec((r, TILE), lambda n: (0, n)) for r, _ in outs],
        grid=(width // TILE,),
        limit=28,
        flops=4 * (X * rows if every else rows) * tokens * width,
    )


def spread_kernel(own_ref, crossed_ref, *out_refs):
    rows = out_refs[0].shape[0]
    for s, out_ref in enumerate(out_refs):
        part = slice(s * rows, (s + 1) * rows)
        total = own_ref[part, :] + decode(crossed_ref[part, :])
        out_ref[...] = encode(total) if s < X - 1 else total


def spread(line, own, crossed):
    width = own.shape[1]
    rows = own.shape[0] // X
    whole = block(X * rows, width)
    return line.run(
        spread_kernel,
        (own, crossed),
        (whole, whole),
        [shape(rows, width, BF16)] * (X - 1) + [shape(rows, width)],
        [block(rows, width)] * X,
        limit=16,
    )


def three(value):
    high = value.astype(BF16).astype(F32)
    rest = value - high
    middle = rest.astype(BF16).astype(F32)
    low = rest - middle
    return jnp.concatenate([high, middle, low, jnp.zeros_like(low)], axis=0).astype(BF16)


def added(parts):
    rows = parts.shape[0] // 4
    return parts[:rows] + (parts[rows : 2 * rows] + parts[2 * rows : 3 * rows])


def edge_kernel(own_ref, next_ref, edge_ref, sums_ref, lowrank_ref):
    differ = own_ref[...].astype(F32) - next_ref[...].astype(F32)
    high = differ.astype(BF16)
    low = (differ - high.astype(F32)).astype(BF16)

    def times(rows, axes):
        parts = three(rows)
        return added(
            lax.dot_general(parts, high, axes, preferred_element_type=F32)
            + lax.dot_general(parts, low, axes, preferred_element_type=F32)
        )

    lowrank = times(edge_ref[...], LAST)
    lowrank_ref[...] = lowrank
    width = differ.shape[1]
    sums_ref[:, :width] = times(lowrank, (((1,), (0,)), ((), ())))
    rank, rows = lowrank.shape
    square = jnp.concatenate([lowrank, jnp.zeros((128 - rank, rows), F32)], axis=0)
    sums_ref[:, width:] = lax.dot_general(lowrank, square, LAST, precision=HIGH, preferred_element_type=F32)


def edge_sums(line, own, following, edge):
    rows, width = own.shape
    rank = edge.shape[0]
    return line.run(
        edge_kernel,
        (own, following, edge),
        (block(rows, width), block(rows, width), block(rank, width)),
        (shape(rank, width + 128), shape(rank, rows)),
        (block(rank, width + 128), block(rank, rows)),
    )


def plus_kernel(one_ref, two_ref, out_ref):
    out_ref[...] = one_ref[...] + two_ref[...]


def plus_ring_kernel(own_ref, one_ref, two_ref, three_ref, out_ref):
    out_ref[...] = (own_ref[...] + two_ref[...]) + (one_ref[...] + three_ref[...])


def combine(line, kernel, *arrays):
    return line.run(
        kernel,
        arrays,
        [block(*array.shape) for array in arrays],
        (shape(*arrays[0].shape),),
        (block(*arrays[0].shape),),
        limit=16,
    )


def solve_kernel(one_ref, two_ref, lowrank_ref, packed_ref):
    rank = lowrank_ref.shape[0]
    width = one_ref.shape[1] - 128
    gram = one_ref[:, width:] + two_ref[:, width:]
    right = one_ref[:, :width] + two_ref[:, :width]
    lowrank = lowrank_ref[...]
    row = lax.broadcasted_iota(jnp.int32, (rank, 1), 0)

    def step(matrix, k, factor, inverse):
        pivot = matrix[k : k + 1, :] * inverse
        return jnp.where(row == k, pivot, matrix - factor * pivot)

    for k in range(rank):
        inverse = 1.0 / jnp.sqrt(gram[k : k + 1, k : k + 1])
        factor = jnp.where(row > k, gram[:, k : k + 1] * inverse, 0.0)
        gram, right, lowrank = (step(m, k, factor, inverse) for m in (gram, right, lowrank))
    packed_ref[:, :width] = right
    packed_ref[:, width:] = lowrank


def solve(line, one, two, lowrank):
    rank, rows = lowrank.shape
    width = one.shape[1] - 128
    return line.run(
        solve_kernel,
        (one, two, lowrank),
        (block(*one.shape), block(*one.shape), block(rank, rows)),
        (shape(rank, width + rows),),
        (block(rank, width + rows),),
        limit=16,
    )


def mix_kernel(weights_ref, right_ref, left_ref, right_basis, left_basis, out_ref, vectors_ref):
    vectors_ref[...] = right_ref[...]

    def parts(value):
        high = value.astype(BF16)
        rest = value - high.astype(F32)
        middle = rest.astype(BF16)
        return high, middle, (rest - middle.astype(F32)).astype(BF16)

    b = parts(jnp.concatenate([right_basis[...], -left_basis[...]], axis=0))
    v = parts(jnp.concatenate([right_ref[...], left_ref[...]], axis=0))
    pairs = ((0, 0), (0, 1), (1, 0), (0, 2), (2, 0), (1, 1))
    approx = lax.dot_general(
        jnp.concatenate([b[i] for i, _ in pairs], axis=0),
        jnp.concatenate([v[j] for _, j in pairs], axis=0),
        (((0,), (0,)), ((), ())),
        preferred_element_type=F32,
    )
    out_ref[...] = weights_ref[...].astype(F32) - gossip_rate * approx


def mix(line, weights, right, left):
    rows, width = weights.shape
    rank = right.shape[0]
    vectors, whole = block(rank, width), block(rows, width)
    basis = block(rank, rows, 0, width // rows)
    return line.run(
        mix_kernel,
        (weights, right, left, right, left),
        (whole, vectors, vectors, basis, basis),
        (shape(rows, width), shape(rank, width)),
        (whole, vectors),
        limit=20,
    )


def finish_kernel(rate, counts, mixed_ref, *refs):
    out_ref = refs[-1]
    start = used = 0
    for count in counts:
        total = refs[used][...]
        for code in refs[used + 1 : used + count]:
            total += decode(code[...])
        part = slice(start, start + total.shape[1])
        out_ref[:, part] = mixed_ref[:, part] - rate * total
        start, used = part.stop, used + count


def finish(line, rate, mixed, parts):
    rows = mixed.shape[0]
    flat = [array for group in parts for array in group]
    whole = block(*mixed.shape)
    return line.run(
        functools.partial(finish_kernel, rate, [len(group) for group in parts]),
        (mixed, *flat),
        (whole, *[block(rows, array.shape[1], array.shape[0] // rows - 1) for array in flat]),
        (shape(*mixed.shape),),
        (whole,),
        limit=20,
    )


def local(context, cotangent, weights, edge_vectors):
    groups = lax.axis_size("fsdp")
    replicas = lax.axis_size("blk")
    context, cotangent, weights, edge = context[0], cotangent[0], weights[0], edge_vectors[0]
    tokens, width = cotangent.shape
    rows = weights.shape[0]
    pair = HALVES * rows
    b_width, a_width = WIDTHS
    a_start, c_start = b_width, b_width + a_width
    c_width = width - c_start

    place = lax.axis_index("fsdp")
    core, x, y = place % 2, (place // 2) % X, place // (2 * X)
    own_place = jnp.stack([core, x, y]).astype(jnp.int32)
    other_place = jnp.stack([1 - core, x, y]).astype(jnp.int32)

    def move(value, target):
        return lax.ppermute(value, "fsdp", [(i, target(i)) for i in range(groups)])

    def flip(bit):
        return lambda i: i ^ bit

    other_core, other_half = flip(1), flip(2 * X)

    def along(by):
        def target(i):
            ahead = by if i % 2 == 0 else X - by
            return i // (2 * X) * (2 * X) + ((i // 2 + ahead) % X) * 2 + i % 2

        return target

    def turn(value, by):
        return lax.ppermute(value, "blk", [(i, (i + by) % replicas) for i in range(replicas)])

    line = Line()

    line.name = "pack1"
    first_lhs, rest_lhs = pack(line, context, other_place, rows)
    line.name = "slice"
    b_other = move(columns(line, cotangent, 0, b_width), other_core)
    first_lhs, rest_lhs = move(first_lhs, other_core), move(rest_lhs, other_core)
    line.name = "pack2"
    parts = [(a_start, a_width), (c_start, c_width)]
    own_lhs, a_cot, c_cot = pack(line, context, own_place, rows, cotangent, parts)
    a_other, c_other = move(a_cot, other_core), move(c_cot, other_core)
    times = functools.partial(product, line, lhs=(own_lhs, first_lhs, rest_lhs), own_cot=cotangent)
    b_part = dict(other_cot=b_other, start=0, rows=pair)
    a_part = dict(other_cot=a_other, start=a_start, rows=pair)
    whole = [(pair, BF16)]
    halves = [(rows, F32), (rows, BF16)]

    line.name = "b0"
    before, left_edge = turn(weights, 1), turn(edge, 1)
    b1 = move(times(first_kernel, **b_part, step=0, outs=whole), along(1))
    rate = learn_rate / math.sqrt(groups * tokens)
    have = {"b1": b1}

    def step_a0():
        have["a1"] = move(times(first_kernel, **a_part, step=0, outs=whole), along(1))

    def step_c():
        outs = [(X * rows, BF16), (X * rows, F32)]
        part = dict(other_cot=c_other, start=c_start, step=None, rows=pair)
        code, have["c_own"] = times(crossed_kernel, **part, outs=outs)
        have["c_cross"] = move(code, other_half)

    def step_edge():
        have["sums"], have["lowrank"] = edge_sums(line, before, weights, left_edge)
        have["sums_core"] = move(have["sums"], other_core)

    def step_add():
        have["sums"] = combine(line, plus_kernel, have["sums"], have["sums_core"])
        have["sums_x"] = [move(have["sums"], flip(2 * by)) for by in (1, 2, 3)]

    def step_sum_x():
        have["sums"] = combine(line, plus_ring_kernel, have["sums"], *have["sums_x"])
        have["sums_y"] = move(have["sums"], other_half)

    def step_solve():
        have["left"] = solve(line, have["sums"], have["sums_y"], have["lowrank"])
        have["right"] = turn(have["left"], -1)

    def step_mix():
        have["mixed"], have["vectors"] = mix(line, weights, have["right"], have["left"])

    def step_ring(name, part, step):
        before, after = f"{name}{step}", f"{name}{step + 1}"
        code = times(relay_kernel, **part, step=step, outs=whole, arrived=have[before])
        have[after] = move(code, along(1))

    def step_settle(name, part):
        keep, send = times(settle_kernel, **part, step=X - 1, outs=halves, arrived=have[f"{name}{X - 1}"])
        have[f"{name}_last"] = keep, move(send, other_half)

    def step_spread():
        *codes, keep = spread(line, have["c_own"], have["c_cross"])
        have["c_last"] = keep, *[move(code, along(X - 1 - s)) for s, code in enumerate(codes)]

    steps = dict(
        a0=step_a0,
        c=step_c,
        edge=step_edge,
        add=step_add,
        sum_x=step_sum_x,
        solve=step_solve,
        mix=step_mix,
        b1=lambda: line.after(left_edge) or step_ring("b", b_part, 1),
        b2=lambda: step_ring("b", b_part, 2),
        b3=lambda: step_settle("b", b_part),
        a1=lambda: step_ring("a", a_part, 1),
        a2=lambda: step_ring("a", a_part, 2),
        a3=lambda: step_settle("a", a_part),
        spread=step_spread,
    )
    for name in ORDER:
        line.name = name
        steps[name]()
    line.name = "finish"
    new_weights = finish(line, rate, have["mixed"], [have["b_last"], have["a_last"], have["c_last"]])
    new_vectors = have["vectors"]
    return (new_weights[None], new_vectors[None])


def solution(mesh):
    return jax.shard_map(
        local,
        mesh=mesh,
        in_specs=(
            P("blk", "fsdp", None),
            P("blk", "fsdp", None),
            P("blk", "fsdp", None),
            P("blk", None, None),
        ),
        out_specs=(P("blk", "fsdp", None), P("blk", None, None)),
        check_vma=False,
    )
```

```python
import functools
import math

import jax
import jax.numpy as jnp
from jax import lax
from jax.experimental import pallas as pl
from jax.experimental.pallas import tpu as pltpu
from jax.sharding import PartitionSpec as P

learn_rate = 0.5
gossip_rate = 0.5

X = 4
HALVES = 2
TILE = 512
POWER = 9
TINY = 1e-37
CODE_SCALE = 2.0**-5

ORDER = ("a0", "c", "b1", "a1", "edge", "b2", "add", "a2", "sum_x", "b3", "solve", "spread", "mix", "a3")
HIGH = lax.Precision.HIGHEST
SHARES = dict(pack1=1.0, slice=1.0, pack2=1.0, b0=30.0, a0=1.0, c=2.0, b1=3.0, b2=3.0)
WIDTHS = (1536, 1536)
F32 = jnp.float32
BF16 = jnp.bfloat16
LAST = (((1,), (1,)), ((), ()))


def encode(total):
    z = total * CODE_SCALE
    z2 = z * z
    z4 = z2 * z2
    return (z4 * z4 * z).astype(BF16)


def decode(code):
    code = code.astype(F32)
    size = jnp.log(jnp.maximum(jnp.abs(code), TINY))
    return code * lax.exp2(size * ((1.0 / POWER - 1.0) / math.log(2.0)) - math.log2(CODE_SCALE))


def shape(rows, width, dtype=F32):
    return jax.ShapeDtypeStruct((rows, width), dtype)


def block(rows, width, row=0, column=0):
    return pl.BlockSpec((rows, width), lambda *_: (row, column))


class Line:
    def __init__(self):
        self.token = None
        self.name = None
        self.extra = []

    def after(self, *arrays):
        self.extra += arrays

    def run(self, kernel, inputs, in_specs, outs, out_specs, grid=(1,), scalars=(), limit=24, flops=0):
        share = SHARES.get(self.name, 10.0)
        inputs, in_specs = list(inputs), list(in_specs)
        size = sum(math.prod(a.shape) * jnp.dtype(a.dtype).itemsize for a in (*inputs, *outs))
        waits = [*self.extra, *([] if self.token is None else [self.token])]
        self.extra, skip = [], len(waits)
        inputs += waits
        in_specs += [pl.BlockSpec(memory_space=pl.ANY)] * skip
        given = len(scalars) + len(inputs)

        def body(*refs):
            kernel(*refs[: given - skip], *refs[given:-1])
            refs[-1][...] = jnp.zeros((8, 128), F32)

        result = pl.pallas_call(
            body,
            grid_spec=pltpu.PrefetchScalarGridSpec(
                num_scalar_prefetch=len(scalars),
                grid=grid,
                in_specs=in_specs,
                out_specs=[*out_specs, block(8, 128)],
            ),
            out_shape=[*outs, shape(8, 128)],
            cost_estimate=pl.CostEstimate(
                flops=int(share * flops), bytes_accessed=int(share * size), transcendentals=0
            ),
            compiler_params=pltpu.CompilerParams(vmem_limit_bytes=limit * 2**20),
        )(*scalars, *inputs)
        *result, self.token = result
        return result[0] if len(outs) == 1 else result


def copy_kernel(in_ref, out_ref):
    out_ref[...] = in_ref[...]


def columns(line, matrix, start, width):
    rows = matrix.shape[0]
    tile = width // 2
    return line.run(
        copy_kernel,
        (matrix,),
        (pl.BlockSpec((rows, tile), lambda n: (0, start // tile + n)),),
        (shape(rows, width, matrix.dtype),),
        (pl.BlockSpec((rows, tile), lambda n: (0, n)),),
        grid=(width // tile,),
    )


def turned(near_ref, far_ref, out_ref):
    rows = near_ref.shape[1]
    out_ref[:rows, :] = near_ref[...].T
    out_ref[rows:, :] = far_ref[...].T


def pack_two_kernel(place_ref, near_ref, far_ref, first_ref, rest_ref):
    step = pl.program_id(0)

    @pl.when(step == 0)
    def _():
        turned(near_ref, far_ref, first_ref)

    @pl.when(step > 0)
    def _():
        turned(near_ref, far_ref, rest_ref)


def pack_kernel(count, place_ref, near_ref, far_ref, *refs):
    turned(near_ref, far_ref, refs[count])
    for part_ref, copy_ref in zip(refs[:count], refs[count + 1 :]):
        copy_ref[...] = part_ref[...]


def pack(line, context, place, rows, cotangent=None, parts=()):
    tokens, width = context.shape

    def column(half, step, place):
        core, x, y = place[0], place[1], place[2]
        turn = jnp.where(core == 0, 2 * X - 1 - step, 1 + step)
        return (0, ((y + half) % HALVES) * (2 * X) + ((x + turn) % X) * 2 + core)

    def taken(start, size):
        tile = size // X
        return pl.BlockSpec((tokens, tile), lambda step, place: (0, start // tile + step))

    pair = 2 * rows
    if parts:
        kernel = functools.partial(pack_kernel, len(parts))
        outs = [shape(X * pair, tokens, BF16)]
        out_specs = [pl.BlockSpec((pair, tokens), lambda step, place: (step, 0))]
    else:
        kernel = pack_two_kernel
        outs = [shape(pair, tokens, BF16), shape((X - 1) * pair, tokens, BF16)]
        out_specs = [
            pl.BlockSpec((pair, tokens), lambda step, place: (0, 0)),
            pl.BlockSpec((pair, tokens), lambda step, place: (jnp.maximum(step - 1, 0), 0)),
        ]
    return line.run(
        kernel,
        (context, context, *[cotangent] * len(parts)),
        (
            pl.BlockSpec((tokens, rows), functools.partial(column, 0)),
            pl.BlockSpec((tokens, rows), functools.partial(column, 1)),
            *[taken(*part) for part in parts],
        ),
        [*outs, *[shape(tokens, size, BF16) for _, size in parts]],
        [*out_specs, *[taken(0, size) for _, size in parts]],
        grid=(X,),
        scalars=(place,),
    )


def both(own_lhs, other_lhs, own_rhs, other_rhs, part=slice(None)):
    total = jnp.dot(own_lhs[...], own_rhs[:, part], preferred_element_type=F32)
    return total + jnp.dot(other_lhs[...], other_rhs[:, part], preferred_element_type=F32)


def parts_of(ref):
    width = ref.shape[1]
    return [slice(start, start + 256) for start in range(0, width, 256)]


def first_kernel(own_lhs, other_lhs, own_rhs, other_rhs, code_ref):
    for part in parts_of(code_ref):
        code_ref[:, part] = encode(both(own_lhs, other_lhs, own_rhs, other_rhs, part))


def relay_kernel(own_lhs, other_lhs, own_rhs, other_rhs, arrived_ref, code_ref):
    for part in parts_of(code_ref):
        total = both(own_lhs, other_lhs, own_rhs, other_rhs, part) + decode(arrived_ref[:, part])
        code_ref[:, part] = encode(total)


def settle_kernel(own_lhs, other_lhs, own_rhs, other_rhs, arrived_ref, keep_ref, code_ref):
    rows = keep_ref.shape[0]
    for part in parts_of(code_ref):
        total = both(own_lhs, other_lhs, own_rhs, other_rhs, part) + decode(arrived_ref[:, part])
        keep_ref[:, part] = total[:rows]
        code_ref[:, part] = encode(total[rows:])


def crossed_kernel(own_lhs, other_lhs, own_rhs, other_rhs, rest_lhs, code_ref, out_ref):
    total = jnp.dot(own_lhs[...], own_rhs[...], preferred_element_type=F32)
    pair = other_lhs.shape[0]
    rows = pair // 2
    for s in range(X):
        lhs = other_lhs[...] if s == 0 else rest_lhs[(s - 1) * pair : s * pair, :]
        both_tokens = total[s * pair : (s + 1) * pair] + jnp.dot(
            lhs, other_rhs[...], preferred_element_type=F32
        )
        out_ref[s * rows : (s + 1) * rows, :] = both_tokens[:rows]
        code_ref[s * rows : (s + 1) * rows, :] = encode(both_tokens[rows:])


def product(line, kernel, lhs, own_cot, other_cot, start, step, rows, outs, arrived=None):
    tokens, width = other_cot.shape
    own_lhs, first_lhs, rest_lhs = lhs
    other_lhs, other_step = (rest_lhs, step - 1) if step else (first_lhs, 0)
    every = step is None
    inputs = [own_lhs, other_lhs, own_cot, other_cot]
    specs = [
        block(*own_lhs.shape) if every else block(rows, tokens, step),
        block(rows, tokens, other_step),
        pl.BlockSpec((tokens, TILE), lambda n: (0, start // TILE + n)),
        pl.BlockSpec((tokens, TILE), lambda n: (0, n)),
    ]
    if every:
        inputs.append(rest_lhs)
        specs.append(block(*rest_lhs.shape))
    if arrived is not None:
        inputs.append(arrived)
        specs.append(pl.BlockSpec((rows, TILE), lambda n: (0, n)))
    return line.run(
        kernel,
        inputs,
        specs,
        [shape(r, width, t) for r, t in outs],
        [pl.BlockSpec((r, TILE), lambda n: (0, n)) for r, _ in outs],
        grid=(width // TILE,),
        limit=28,
        flops=4 * (X * rows if every else rows) * tokens * width,
    )


def spread_kernel(own_ref, crossed_ref, *out_refs):
    rows = out_refs[0].shape[0]
    for s, out_ref in enumerate(out_refs):
        part = slice(s * rows, (s + 1) * rows)
        total = own_ref[part, :] + decode(crossed_ref[part, :])
        out_ref[...] = encode(total) if s < X - 1 else total


def spread(line, own, crossed):
    width = own.shape[1]
    rows = own.shape[0] // X
    whole = block(X * rows, width)
    return line.run(
        spread_kernel,
        (own, crossed),
        (whole, whole),
        [shape(rows, width, BF16)] * (X - 1) + [shape(rows, width)],
        [block(rows, width)] * X,
        limit=16,
    )


def three(value):
    high = value.astype(BF16).astype(F32)
    rest = value - high
    middle = rest.astype(BF16).astype(F32)
    low = rest - middle
    return jnp.concatenate([high, middle, low, jnp.zeros_like(low)], axis=0).astype(BF16)


def added(parts):
    rows = parts.shape[0] // 4
    return parts[:rows] + (parts[rows : 2 * rows] + parts[2 * rows : 3 * rows])


def edge_kernel(own_ref, next_ref, edge_ref, sums_ref, lowrank_ref):
    differ = own_ref[...].astype(F32) - next_ref[...].astype(F32)
    high = differ.astype(BF16)
    low = (differ - high.astype(F32)).astype(BF16)

    def times(rows, axes):
        parts = three(rows)
        return added(
            lax.dot_general(parts, high, axes, preferred_element_type=F32)
            + lax.dot_general(parts, low, axes, preferred_element_type=F32)
        )

    lowrank = times(edge_ref[...], LAST)
    lowrank_ref[...] = lowrank
    width = differ.shape[1]
    sums_ref[:, :width] = times(lowrank, (((1,), (0,)), ((), ())))
    rank, rows = lowrank.shape
    square = jnp.concatenate([lowrank, jnp.zeros((128 - rank, rows), F32)], axis=0)
    sums_ref[:, width:] = lax.dot_general(lowrank, square, LAST, precision=HIGH, preferred_element_type=F32)


def edge_sums(line, own, following, edge):
    rows, width = own.shape
    rank = edge.shape[0]
    return line.run(
        edge_kernel,
        (own, following, edge),
        (block(rows, width), block(rows, width), block(rank, width)),
        (shape(rank, width + 128), shape(rank, rows)),
        (block(rank, width + 128), block(rank, rows)),
    )


def plus_kernel(one_ref, two_ref, out_ref):
    out_ref[...] = one_ref[...] + two_ref[...]


def plus_ring_kernel(own_ref, one_ref, two_ref, three_ref, out_ref):
    out_ref[...] = (own_ref[...] + two_ref[...]) + (one_ref[...] + three_ref[...])


def combine(line, kernel, *arrays):
    return line.run(
        kernel,
        arrays,
        [block(*array.shape) for array in arrays],
        (shape(*arrays[0].shape),),
        (block(*arrays[0].shape),),
        limit=16,
    )


def solve_kernel(one_ref, two_ref, lowrank_ref, packed_ref):
    rank = lowrank_ref.shape[0]
    width = one_ref.shape[1] - 128
    gram = one_ref[:, width:] + two_ref[:, width:]
    right = one_ref[:, :width] + two_ref[:, :width]
    lowrank = lowrank_ref[...]
    row = lax.broadcasted_iota(jnp.int32, (rank, 1), 0)

    def step(matrix, k, factor, inverse):
        pivot = matrix[k : k + 1, :] * inverse
        return jnp.where(row == k, pivot, matrix - factor * pivot)

    for k in range(rank):
        inverse = 1.0 / jnp.sqrt(gram[k : k + 1, k : k + 1])
        factor = jnp.where(row > k, gram[:, k : k + 1] * inverse, 0.0)
        gram, right, lowrank = (step(m, k, factor, inverse) for m in (gram, right, lowrank))
    packed_ref[:, :width] = right
    packed_ref[:, width:] = lowrank


def solve(line, one, two, lowrank):
    rank, rows = lowrank.shape
    width = one.shape[1] - 128
    return line.run(
        solve_kernel,
        (one, two, lowrank),
        (block(*one.shape), block(*one.shape), block(rank, rows)),
        (shape(rank, width + rows),),
        (block(rank, width + rows),),
        limit=16,
    )


def mix_kernel(weights_ref, right_ref, left_ref, right_basis, left_basis, out_ref, vectors_ref):
    vectors_ref[...] = right_ref[...]

    def parts(value):
        high = value.astype(BF16)
        rest = value - high.astype(F32)
        middle = rest.astype(BF16)
        return high, middle, (rest - middle.astype(F32)).astype(BF16)

    b = parts(jnp.concatenate([right_basis[...], -left_basis[...]], axis=0))
    v = parts(jnp.concatenate([right_ref[...], left_ref[...]], axis=0))
    pairs = ((0, 0), (0, 1), (1, 0), (0, 2), (2, 0), (1, 1))
    approx = lax.dot_general(
        jnp.concatenate([b[i] for i, _ in pairs], axis=0),
        jnp.concatenate([v[j] for _, j in pairs], axis=0),
        (((0,), (0,)), ((), ())),
        preferred_element_type=F32,
    )
    out_ref[...] = weights_ref[...].astype(F32) - gossip_rate * approx


def mix(line, weights, right, left):
    rows, width = weights.shape
    rank = right.shape[0]
    vectors, whole = block(rank, width), block(rows, width)
    basis = block(rank, rows, 0, width // rows)
    return line.run(
        mix_kernel,
        (weights, right, left, right, left),
        (whole, vectors, vectors, basis, basis),
        (shape(rows, width), shape(rank, width)),
        (whole, vectors),
        limit=20,
    )


def finish_kernel(rate, counts, mixed_ref, *refs):
    out_ref = refs[-1]
    start = used = 0
    for count in counts:
        total = refs[used][...]
        for code in refs[used + 1 : used + count]:
            total += decode(code[...])
        part = slice(start, start + total.shape[1])
        out_ref[:, part] = mixed_ref[:, part] - rate * total
        start, used = part.stop, used + count


def finish(line, rate, mixed, parts):
    rows = mixed.shape[0]
    flat = [array for group in parts for array in group]
    whole = block(*mixed.shape)
    return line.run(
        functools.partial(finish_kernel, rate, [len(group) for group in parts]),
        (mixed, *flat),
        (whole, *[block(rows, array.shape[1], array.shape[0] // rows - 1) for array in flat]),
        (shape(*mixed.shape),),
        (whole,),
        limit=20,
    )


def local(context, cotangent, weights, edge_vectors):
    groups = lax.axis_size("fsdp")
    replicas = lax.axis_size("blk")
    context, cotangent, weights, edge = context[0], cotangent[0], weights[0], edge_vectors[0]
    tokens, width = cotangent.shape
    rows = weights.shape[0]
    pair = HALVES * rows
    b_width, a_width = WIDTHS
    a_start, c_start = b_width, b_width + a_width
    c_width = width - c_start

    place = lax.axis_index("fsdp")
    core, x, y = place % 2, (place // 2) % X, place // (2 * X)
    own_place = jnp.stack([core, x, y]).astype(jnp.int32)
    other_place = jnp.stack([1 - core, x, y]).astype(jnp.int32)

    def move(value, target):
        return lax.ppermute(value, "fsdp", [(i, target(i)) for i in range(groups)])

    def flip(bit):
        return lambda i: i ^ bit

    other_core, other_half = flip(1), flip(2 * X)

    def along(by):
        def target(i):
            ahead = by if i % 2 == 0 else X - by
            return i // (2 * X) * (2 * X) + ((i // 2 + ahead) % X) * 2 + i % 2

        return target

    def turn(value, by):
        return lax.ppermute(value, "blk", [(i, (i + by) % replicas) for i in range(replicas)])

    line = Line()

    line.name = "pack1"
    first_lhs, rest_lhs = pack(line, context, other_place, rows)
    line.name = "slice"
    b_other = move(columns(line, cotangent, 0, b_width), other_core)
    first_lhs, rest_lhs = move(first_lhs, other_core), move(rest_lhs, other_core)
    line.name = "pack2"
    parts = [(a_start, a_width), (c_start, c_width)]
    own_lhs, a_cot, c_cot = pack(line, context, own_place, rows, cotangent, parts)
    a_other, c_other = move(a_cot, other_core), move(c_cot, other_core)
    times = functools.partial(product, line, lhs=(own_lhs, first_lhs, rest_lhs), own_cot=cotangent)
    b_part = dict(other_cot=b_other, start=0, rows=pair)
    a_part = dict(other_cot=a_other, start=a_start, rows=pair)
    whole = [(pair, BF16)]
    halves = [(rows, F32), (rows, BF16)]

    line.name = "b0"
    before, left_edge = turn(weights, 1), turn(edge, 1)
    b1 = move(times(first_kernel, **b_part, step=0, outs=whole), along(1))
    rate = learn_rate / math.sqrt(groups * tokens)
    have = {"b1": b1}

    def step_a0():
        have["a1"] = move(times(first_kernel, **a_part, step=0, outs=whole), along(1))

    def step_c():
        outs = [(X * rows, BF16), (X * rows, F32)]
        part = dict(other_cot=c_other, start=c_start, step=None, rows=pair)
        code, have["c_own"] = times(crossed_kernel, **part, outs=outs)
        have["c_cross"] = move(code, other_half)

    def step_edge():
        have["sums"], have["lowrank"] = edge_sums(line, before, weights, left_edge)
        have["sums_core"] = move(have["sums"], other_core)

    def step_add():
        have["sums"] = combine(line, plus_kernel, have["sums"], have["sums_core"])
        have["sums_x"] = [move(have["sums"], flip(2 * by)) for by in (1, 2, 3)]

    def step_sum_x():
        have["sums"] = combine(line, plus_ring_kernel, have["sums"], *have["sums_x"])
        have["sums_y"] = move(have["sums"], other_half)

    def step_solve():
        have["left"] = solve(line, have["sums"], have["sums_y"], have["lowrank"])
        have["right"] = turn(have["left"], -1)

    def step_mix():
        have["mixed"], have["vectors"] = mix(line, weights, have["right"], have["left"])

    def step_ring(name, part, step):
        before, after = f"{name}{step}", f"{name}{step + 1}"
        code = times(relay_kernel, **part, step=step, outs=whole, arrived=have[before])
        have[after] = move(code, along(1))

    def step_settle(name, part):
        keep, send = times(settle_kernel, **part, step=X - 1, outs=halves, arrived=have[f"{name}{X - 1}"])
        have[f"{name}_last"] = keep, move(send, other_half)

    def step_spread():
        *codes, keep = spread(line, have["c_own"], have["c_cross"])
        have["c_last"] = keep, *[move(code, along(X - 1 - s)) for s, code in enumerate(codes)]

    steps = dict(
        a0=step_a0,
        c=step_c,
        edge=step_edge,
        add=step_add,
        sum_x=step_sum_x,
        solve=step_solve,
        mix=step_mix,
        b1=lambda: line.after(left_edge) or step_ring("b", b_part, 1),
        b2=lambda: step_ring("b", b_part, 2),
        b3=lambda: step_settle("b", b_part),
        a1=lambda: step_ring("a", a_part, 1),
        a2=lambda: step_ring("a", a_part, 2),
        a3=lambda: step_settle("a", a_part),
        spread=step_spread,
    )
    for name in ORDER:
        line.name = name
        steps[name]()
    line.name = "finish"
    new_weights = finish(line, rate, have["mixed"], [have["b_last"], have["a_last"], have["c_last"]])
    new_vectors = have["vectors"]
    return (new_weights[None], new_vectors[None])


def solution(mesh):
    return jax.shard_map(
        local,
        mesh=mesh,
        in_specs=(
            P("blk", "fsdp", None),
            P("blk", "fsdp", None),
            P("blk", "fsdp", None),
            P("blk", None, None),
        ),
        out_specs=(P("blk", "fsdp", None), P("blk", None, None)),
        check_vma=False,
    )
```
